32 devices in a mesh: parts: 2 (over x), store: 16 (over z, y, core).
Axes of the slice: x: 2, y: 2, z: 4, core: 2. Of those that a mesh axis runs over, the one named last changes fastest.
Arguments:
- rows_in: bfloat16 [128, 40, 8192], P(('parts', 'store')), parts along dimension 0, may hold values from -6 to 6
- norm_gain: bfloat16 [8192], replicated, may hold values from 0.099609375 to 1.8984375
- kv_weight: bfloat16 [8192, 1024], P('store'), may hold values from -0.0625 to 0.0625
- queries: bfloat16 [128, 40, 4096], P(('parts', 'store')), parts along dimension 0, may hold values from -8 to 8
- store_pages: bfloat16 [128, 16, 2, 512], P(('parts', 'store')), parts along dimension 0, may hold values from -8 to 8
- passage_home: int32 [128], P('parts'), parts along dimension 0, may hold values from 0 to 63, as said below
- passage_ids: int32 [128, 20], P('parts'), parts along dimension 0, may hold values from 0 to 63, as said below
- passage_count: int32 [128], P(('parts', 'store')), parts along dimension 0, may hold values from 6 to 20
- recompute_rows: int32 [128, 20, 2], P('parts'), parts along dimension 0, may hold values from 0 to 15, as said below
Outputs:
- attended: bfloat16 [128, 40, 4096], P(('parts', 'store')), parts along dimension 0
The draws below stay inside these ranges and needn't reach their ends.
There are 2 independent parts, one for each index of `parts`. The reference program is written for one: setup_inputs(seed, part) draws one part's arguments, and reference() takes and returns one part's arrays. A program takes and returns all parts, laid end to end along the dimension named above; an argument that names none is the same for every part. Nothing has to cross between parts.
Inputs may be any that keep to these rules, and one draw needn't show every extreme that they name: `passage_home`: A permutation. `passage_ids`: over all slots of the 4 requests of one device, at most 5 name passages held in the rows of one device's block of store_pages; some device pair reaches 5. Unused slots name passages too. `recompute_rows`: the 2 rows of one passage slot differ.
All inputs are finite; a program needn't handle non-finite values.
Results may differ from the reference program's by a relative error of at most 0.0055.
Values may be sent and summed in bfloat16 or wider, within the bound.
No kernel may reach another device: no remote copies, remote signals or barrier semaphores. Data moves between devices by JAX's collectives and lax.ppermute only.
A program may use at most 128 MiB of HBM per device.

```python
import math
import jax
import jax.numpy as jnp
from jax import lax

D = 8192
QUERY_HEADS = 32
KEY_VALUE_HEADS = 4
HEAD_SIZE = 128
KVW = 512
PLEN = 16
SEL_P = 2
MAXP = 20
R_DEV = 4
P_DEV = 4
REQS = 64
PASSAGES = 64
CONTEXT_SLOTS = 320
REDONE_ROWS = 40
N_STORE = 16


def placement_tables(key):
    key = jax.random.fold_in(key, 7)
    parts_keys = jax.random.split(key, 4)
    home = jax.random.permutation(parts_keys[0], PASSAGES)
    holder = jnp.argsort(home)
    positions = R_DEV * MAXP

    def shuffle_shards(inner):
        return jax.random.permutation(inner, N_STORE)

    def shuffle_positions(inner):
        return jax.random.permutation(inner, positions)
    order = jax.vmap(shuffle_shards)(jax.random.split(parts_keys[1], N_STORE))
    spread = jax.vmap(shuffle_positions)(jax.random.split(parts_keys[2], N_STORE)) % N_STORE
    shard = jnp.take_along_axis(order, spread, axis=1)
    local = jax.random.randint(parts_keys[3], (N_STORE, positions), 0, P_DEV)
    ids = holder[shard * P_DEV + local].reshape(REQS, MAXP)
    return (home.astype(jnp.int32), ids.astype(jnp.int32))


def draw_passage_home(key, part):
    return placement_tables(key)[0]


def draw_passage_ids(key, part):
    return placement_tables(key)[1]


def draw_recompute_rows(key, part):
    key = jax.random.fold_in(key, 3)

    def pick_rows(inner):
        return jax.random.permutation(inner, PLEN)[:SEL_P]
    rows = jax.vmap(pick_rows)(jax.random.split(key, REQS * MAXP))
    return rows.reshape(REQS, MAXP, SEL_P).astype(jnp.int32)


def draw_queries(key, part):
    key = jax.random.fold_in(key, 1)
    subkeys = jax.random.split(key, 2)
    value_matrix = jax.random.truncated_normal(subkeys[1], -6.0, 6.0, (REQS, REDONE_ROWS, QUERY_HEADS * HEAD_SIZE))
    return value_matrix.astype(jnp.bfloat16)


def draw_store_pages(key, part):
    key = jax.random.fold_in(key, 2)
    subkeys = jax.random.split(key, 2)
    value_matrix = jax.random.truncated_normal(subkeys[1], -6.0, 6.0, (PASSAGES, PLEN, 2, KVW))
    return value_matrix.astype(jnp.bfloat16)


def place_ends(entries, stream_key, least, high):
    index_at = [jax.random.randint(jax.random.fold_in(stream_key, axis), (), 0, length) for axis, length in enumerate(entries.shape)]
    widest = entries.shape.index(max(entries.shape))
    neighbour = index_at[:widest] + [(index_at[widest] + 1) % entries.shape[widest]] + index_at[widest + 1:]
    return entries.at[tuple(index_at)].set(least).at[tuple(neighbour)].set(high)


def steps_of(key, dims, shards, least, largest):
    level, own = 1.0, jax.random.fold_in(key, 6)
    for dim, blocks in shards:
        heights = jnp.exp(jax.random.uniform(jax.random.fold_in(own, dim), (blocks,), jnp.float32, least / len(shards), largest / len(shards)))
        level = level * jnp.repeat(heights, dims[dim] // blocks).reshape([-1 if axis == dim else 1 for axis in range(len(dims))])
    return level


def normal_values(key, shape, deviation, reach, pieces=(), held_as=jnp.bfloat16):
    level = steps_of(key, shape, pieces, -0.22, 0.18) if pieces else 1.0
    values = jax.random.normal(key, shape, jnp.float32) * deviation * level
    return jnp.minimum(jnp.maximum(values, -reach), reach).astype(held_as)


def setup_inputs(seed: int = 0, part: int = 0) -> dict:
    keys = jax.random.split(jax.random.key(seed), 10)
    own_keys = jax.random.split(jax.random.fold_in(keys[9], part), 10)
    return {
        "rows_in": normal_values(own_keys[0], (REQS, REDONE_ROWS, D), 1.0, 6.0, ((0, 16),)),
        "norm_gain": jnp.clip(1.0 + 0.18 * jax.random.normal(keys[1], (D,), jnp.float32), 0.099609375, 1.8984375).astype(jnp.bfloat16),
        "kv_weight": normal_values(keys[2], (D, 2 * KVW), D ** -0.5, 0.0625, ((0, 16),)),
        "queries": draw_queries(jax.random.fold_in(jax.random.fold_in(keys[9], part), 71), part),
        "store_pages": draw_store_pages(jax.random.fold_in(jax.random.fold_in(keys[9], part), 71), part),
        "passage_home": draw_passage_home(jax.random.fold_in(jax.random.fold_in(keys[9], part), 71), part),
        "passage_ids": draw_passage_ids(jax.random.fold_in(jax.random.fold_in(keys[9], part), 71), part),
        "passage_count": place_ends(jax.random.randint(own_keys[7], (REQS,), 6, MAXP + 1), jax.random.fold_in(own_keys[7], 1), 6, MAXP).astype(jnp.int32),
        "recompute_rows": draw_recompute_rows(jax.random.fold_in(jax.random.fold_in(keys[9], part), 71), part),
    }


def reference(rows_in, norm_gain, kv_weight, queries, store_pages, passage_home, passage_ids, passage_count, recompute_rows):
    query_group = QUERY_HEADS // KEY_VALUE_HEADS
    scale = 1.0 / math.sqrt(HEAD_SIZE)
    key_pos = jnp.arange(CONTEXT_SLOTS, dtype=jnp.int32)
    key_slot = key_pos // PLEN
    query_slot = jnp.arange(REDONE_ROWS, dtype=jnp.int32) // SEL_P
    gain = norm_gain.astype(jnp.float32)

    def single(items):
        inputs, query_matrix, ids, count, rows = items
        wide = inputs.astype(jnp.float32)
        normed = (wide * lax.rsqrt(lax.optimization_barrier(jnp.mean(wide * wide, axis=-1, keepdims=True)) + 1e-05) * gain).astype(jnp.bfloat16)
        fresh = jnp.dot(normed, kv_weight, preferred_element_type=jnp.float32).astype(jnp.bfloat16)
        fresh = fresh.reshape(MAXP, SEL_P, 2, KVW)
        cached = store_pages[passage_home[ids]]
        onehot = rows[:, :, None] == jnp.arange(PLEN, dtype=jnp.int32)[None, None, :]
        placed = jnp.einsum('mij,mick->mjck', onehot.astype(jnp.float32), fresh.astype(jnp.float32))
        touched = jnp.any(onehot, axis=1)
        patched_cache = jnp.where(touched[:, :, None, None], placed.astype(jnp.bfloat16), cached).reshape(CONTEXT_SLOTS, 2, KVW)
        key_matrix = patched_cache[:, 0].reshape(CONTEXT_SLOTS, KEY_VALUE_HEADS, HEAD_SIZE)
        value_matrix = patched_cache[:, 1].reshape(CONTEXT_SLOTS, KEY_VALUE_HEADS, HEAD_SIZE)
        head_count = query_matrix.reshape(REDONE_ROWS, KEY_VALUE_HEADS, query_group, HEAD_SIZE)
        scores = jnp.einsum('qhgd,khd->hgqk', head_count.astype(jnp.float32), key_matrix.astype(jnp.float32)) * scale
        query_pos = query_slot * PLEN + rows.reshape(REDONE_ROWS)
        visible = (key_slot[None, :] < count) & (key_pos[None, :] <= query_pos[:, None])
        scores = jnp.where(visible[None, None], scores, -1e+30)
        top = lax.optimization_barrier(jnp.max(scores, axis=-1, keepdims=True))
        expd = jnp.exp(scores - top)
        weights = (expd / lax.optimization_barrier(jnp.sum(expd, axis=-1, keepdims=True))).astype(jnp.bfloat16)
        result = jnp.einsum('hgqk,khd->qhgd', weights.astype(jnp.float32), value_matrix.astype(jnp.float32)).reshape(REDONE_ROWS, QUERY_HEADS * HEAD_SIZE)
        result = jnp.where((query_slot < count)[:, None], result, 0.0)
        return result.astype(jnp.bfloat16)
    return lax.map(single, (rows_in, queries, passage_ids, passage_count, recompute_rows))
```

```python
import functools
import math

import jax
import jax.numpy as jnp
from jax import lax
from jax.experimental import pallas as pl
from jax.experimental.pallas import tpu as pltpu
from jax.sharding import PartitionSpec as P

QUERY_HEADS = 32
KEY_VALUE_HEADS = 4
HEAD_SIZE = 128
HEAD_GROUP = QUERY_HEADS // KEY_VALUE_HEADS
GROUP = 4
HIDDEN = -1e30
EXP2_SCALE = math.log2(math.e) / math.sqrt(HEAD_SIZE)
VMEM_LIMIT = 48 * 2**20


def params(**more):
    return pltpu.CompilerParams(vmem_limit_bytes=VMEM_LIMIT, **more)


def whole():
    return pl.BlockSpec(memory_space=pltpu.VMEM)


def smem():
    return pl.BlockSpec(memory_space=pltpu.SMEM)


def send(x, steps):
    shards = lax.axis_size("store")
    pairs = [(i, (i + steps * GROUP) % shards) for i in range(shards)]
    return lax.ppermute(x, "store", pairs)


def flip(x, bits):
    pairs = [(i, i ^ bits) for i in range(lax.axis_size("store"))]
    return lax.ppermute(x, "store", pairs)


def swap(x):
    return lax.ppermute(x, "parts", [(0, 1), (1, 0)])


def norm_kernel(chunk, chunks, offs_ref, rows_ref, gain_ref, o0, o1, o2, o3, held):
    wide = rows_ref[...].astype(jnp.float32)
    inv = lax.rsqrt(jnp.mean(wide * wide, axis=-1, keepdims=True) + 1e-05)
    held[...] = (wide * inv * gain_ref[...].astype(jnp.float32)).astype(jnp.bfloat16)
    for j, out in enumerate((o0, o1, o2, o3)):
        for k in range(chunks):
            at = pl.multiple_of(offs_ref[j * chunks + k] * 128, 128)
            out[:, k * chunk : (k + 1) * chunk] = held[:, pl.ds(at, chunk)]


def norm_rows(rows, gain, offs, chunk):
    count, width = rows.shape
    chunks = width // GROUP // chunk
    block = 32
    out = jax.ShapeDtypeStruct((count, width // GROUP), jnp.bfloat16)
    return pl.pallas_call(
        functools.partial(norm_kernel, chunk, chunks),
        out_shape=[out] * GROUP,
        grid=(count // block,),
        in_specs=[
            smem(),
            pl.BlockSpec((block, width), lambda i: (i, 0)),
            pl.BlockSpec((1, width), lambda i: (0, 0)),
        ],
        out_specs=[pl.BlockSpec((block, width // GROUP), lambda i: (i, 0))] * GROUP,
        scratch_shapes=[pltpu.VMEM((block, width), jnp.bfloat16)],
        compiler_params=params(),
        cost_estimate=pl.CostEstimate(
            flops=6 * count * width, bytes_accessed=4 * count * width, transcendentals=0
        ),
        name="norm",
    )(offs, rows, gain.reshape(1, width))


def dot(a, b):
    return jnp.dot(a, b, preferred_element_type=jnp.float32)


def first_kernel(a0, a1, a2, a3, w0, w1, w2, w3, w4, acc):
    rows = a0.shape[0]
    for j, a in enumerate((a0, a1, a2, a3)):
        total = None
        at = 0
        for w in (w0, w1, w2, w3, w4):
            depth = w.shape[0]
            term = dot(a[:, at : at + depth], w[...])
            total = term if total is None else total + term
            at += depth
        acc[j * rows : (j + 1) * rows, :] = total


def first_part(acts, weights):
    rows, depth = acts[0].shape
    features = weights[0].shape[1]
    block = 256
    used = sum(w.shape[0] for w in weights)
    return pl.pallas_call(
        first_kernel,
        out_shape=jax.ShapeDtypeStruct((GROUP * rows, features), jnp.float32),
        grid=(features // block,),
        in_specs=[pl.BlockSpec((rows, used), lambda i: (0, 0))] * GROUP
        + [pl.BlockSpec((w.shape[0], block), lambda i: (0, i)) for w in weights],
        out_specs=pl.BlockSpec((GROUP * rows, block), lambda i: (0, i)),
        compiler_params=params(),
        cost_estimate=pl.CostEstimate(
            flops=2 * GROUP * rows * used * features,
            bytes_accessed=2 * used * (GROUP * rows + features) + 4 * GROUP * rows * features,
            transcendentals=0,
        ),
        name="first_part",
    )(*acts, *weights)


def second_kernel(a0, a1, a2, a3, w0, w1, w2, w3, acc, keep, send):
    rows = a0.shape[0]
    for j, a in enumerate((a0, a1, a2, a3)):
        total = acc[j * rows : (j + 1) * rows, :]
        at = 0
        for w in (w0, w1, w2, w3):
            depth = w.shape[0]
            total = total + dot(a[:, at : at + depth], w[...])
            at += depth
        place = slice((j // 2) * rows, (j // 2 + 1) * rows)
        if j % 2:
            send[place, :] = total.astype(jnp.bfloat16)
        else:
            keep[place, :] = total


def second_part(acts, weights, acc):
    rows, depth = acts[0].shape
    features = weights[0].shape[1]
    block = 256
    used = sum(w.shape[0] for w in weights)
    last = depth // used - 1
    return pl.pallas_call(
        second_kernel,
        out_shape=[
            jax.ShapeDtypeStruct((2 * rows, features), jnp.float32),
            jax.ShapeDtypeStruct((2 * rows, features), jnp.bfloat16),
        ],
        grid=(features // block,),
        in_specs=[pl.BlockSpec((rows, used), lambda i: (0, last))] * GROUP
        + [pl.BlockSpec((w.shape[0], block), lambda i: (0, i)) for w in weights]
        + [pl.BlockSpec((GROUP * rows, block), lambda i: (0, i))],
        out_specs=[pl.BlockSpec((2 * rows, block), lambda i: (0, i))] * 2,
        compiler_params=params(),
        cost_estimate=pl.CostEstimate(
            flops=2 * GROUP * rows * used * features,
            bytes_accessed=2 * used * (GROUP * rows + features) + 7 * GROUP * rows * features,
            transcendentals=0,
        ),
        name="second_part",
    )(*acts, *weights, acc)


def stacked_queries(q_ref, head):
    parts = []
    for i in range(HEAD_GROUP):
        at = (head * HEAD_GROUP + i) * HEAD_SIZE
        parts.append(q_ref[0, :, at : at + HEAD_SIZE].astype(jnp.float32))
    return jnp.concatenate(parts, axis=0).astype(jnp.bfloat16)


def scores_of(q, keys, bias):
    s = lax.dot_general(q, keys, (((1,), (1,)), ((), ())), preferred_element_type=jnp.float32)
    rows, cols = bias.shape
    s = (s * EXP2_SCALE).reshape(HEAD_GROUP, rows, cols) + bias[None]
    return s.reshape(HEAD_GROUP * rows, cols)


def cached_kernel(
    per_dev, place_ref, home_ref, ids_ref, q_ref, near_ref, far_ref, bias_ref,
    out_ref, stat_ref, pages, context, sems,
):
    r = pl.program_id(0)
    rows = near_ref.shape[0]
    plen = context.shape[0] // ids_ref.shape[1]

    @pl.when(r == 0)
    def _():
        one = pltpu.make_async_copy(near_ref, pages.at[pl.ds(0, rows)], sems.at[0])
        two = pltpu.make_async_copy(far_ref, pages.at[pl.ds(rows, rows)], sems.at[1])
        one.start()
        two.start()
        one.wait()
        two.wait()

    for m in range(ids_ref.shape[1]):
        slot = home_ref[ids_ref[r, m]]
        position = place_ref[slot // per_dev] * per_dev + slot % per_dev
        at = pl.multiple_of(position * plen, plen)
        context[m * plen : (m + 1) * plen, :] = pages[pl.ds(at, plen), :]
    bias = bias_ref[0]
    kvw = KEY_VALUE_HEADS * HEAD_SIZE
    lane = lax.broadcasted_iota(jnp.int32, (HEAD_GROUP * bias.shape[0], HEAD_SIZE), 1)
    for g in range(KEY_VALUE_HEADS):
        q = stacked_queries(q_ref, g)
        keys = context[:, g * HEAD_SIZE : (g + 1) * HEAD_SIZE]
        values = context[:, kvw + g * HEAD_SIZE : kvw + (g + 1) * HEAD_SIZE]
        s = scores_of(q, keys, bias)
        top = jnp.max(s, axis=-1, keepdims=True)
        e = jnp.exp2(s - top)
        total = jnp.sum(e, axis=-1, keepdims=True)
        out_ref[0, g] = dot(e.astype(jnp.bfloat16), values)
        stat_ref[0, g] = jnp.where(lane < HEAD_SIZE // 2, top, total)


def cached_attention(per_dev, place, home, ids, near, far, queries, bias):
    owned, rows, width = queries.shape
    context = bias.shape[2]
    stacked = HEAD_GROUP * rows
    state = jax.ShapeDtypeStruct((owned, KEY_VALUE_HEADS, stacked, HEAD_SIZE), jnp.float32)
    state_spec = pl.BlockSpec((1, KEY_VALUE_HEADS, stacked, HEAD_SIZE), lambda r: (r, 0, 0, 0))
    return pl.pallas_call(
        functools.partial(cached_kernel, per_dev),
        out_shape=[state, state],
        grid=(owned,),
        in_specs=[
            smem(),
            smem(),
            smem(),
            pl.BlockSpec((1, rows, width), lambda r: (r, 0, 0)),
            pl.BlockSpec(memory_space=pl.ANY),
            pl.BlockSpec(memory_space=pl.ANY),
            pl.BlockSpec((1, rows, context), lambda r: (r, 0, 0)),
        ],
        out_specs=[state_spec, state_spec],
        scratch_shapes=[
            pltpu.VMEM((2 * near.shape[0], near.shape[1]), jnp.bfloat16),
            pltpu.VMEM((context, near.shape[1]), jnp.bfloat16),
            pltpu.SemaphoreType.DMA((2,)),
        ],
        compiler_params=params(),
        cost_estimate=pl.CostEstimate(
            flops=4 * owned * rows * width * context,
            bytes_accessed=4 * near.size + 2 * queries.size + 8 * owned * stacked * 4 * HEAD_SIZE,
            transcendentals=owned * rows * QUERY_HEADS * context,
        ),
        name="cached_attention",
    )(place, home, ids, queries, near, far, bias)


def fresh_kernel(maxp, count_ref, q_ref, own_ref, core_ref, y_ref, bias_ref, part_ref, stat_ref, out_ref):
    r = pl.program_id(0)
    fresh = (
        own_ref[0] + core_ref[0].astype(jnp.float32) + y_ref[0].astype(jnp.float32)
    ).astype(jnp.bfloat16)
    bias = bias_ref[0]
    rows = bias.shape[0]
    kvw = KEY_VALUE_HEADS * HEAD_SIZE
    per_pass = rows // maxp
    slot = lax.broadcasted_iota(jnp.int32, (rows, HEAD_SIZE), 0) // per_pass
    live = slot < count_ref[r]
    for g in range(KEY_VALUE_HEADS):
        q = stacked_queries(q_ref, g)
        keys = fresh[:, g * HEAD_SIZE : (g + 1) * HEAD_SIZE]
        values = fresh[:, kvw + g * HEAD_SIZE : kvw + (g + 1) * HEAD_SIZE]
        s = scores_of(q, keys, bias)
        top1 = stat_ref[0, g, :, 0:1]
        sum1 = stat_ref[0, g, :, HEAD_SIZE // 2 : HEAD_SIZE // 2 + 1]
        top = jnp.maximum(top1, jnp.max(s, axis=-1, keepdims=True))
        e = jnp.exp2(s - top)
        keep = jnp.exp2(top1 - top)
        inv = 1.0 / (sum1 * keep + jnp.sum(e, axis=-1, keepdims=True))
        result = (part_ref[0, g] * keep + dot(e.astype(jnp.bfloat16), values)) * inv
        for i in range(HEAD_GROUP):
            at = (g * HEAD_GROUP + i) * HEAD_SIZE
            one = result[i * rows : (i + 1) * rows]
            out_ref[0, :, at : at + HEAD_SIZE] = jnp.where(live, one, 0.0).astype(jnp.bfloat16)


def fresh_attention(maxp, count, queries, own, core, y, bias, part, stat):
    owned, rows, width = queries.shape
    features = own.shape[-1]
    stacked = HEAD_GROUP * rows
    state_spec = pl.BlockSpec((1, KEY_VALUE_HEADS, stacked, HEAD_SIZE), lambda r: (r, 0, 0, 0))
    row_spec = pl.BlockSpec((1, rows, features), lambda r: (r, 0, 0))
    query_spec = pl.BlockSpec((1, rows, width), lambda r: (r, 0, 0))
    return pl.pallas_call(
        functools.partial(fresh_kernel, maxp),
        out_shape=jax.ShapeDtypeStruct(queries.shape, jnp.bfloat16),
        grid=(owned,),
        in_specs=[
            smem(),
            query_spec,
            row_spec,
            row_spec,
            row_spec,
            pl.BlockSpec((1, rows, rows), lambda r: (r, 0, 0)),
            state_spec,
            state_spec,
        ],
        out_specs=query_spec,
        compiler_params=params(),
        cost_estimate=pl.CostEstimate(
            flops=4 * owned * rows * width * rows,
            bytes_accessed=4 * queries.size + 8 * part.size,
            transcendentals=owned * rows * QUERY_HEADS * rows,
        ),
        name="fresh_attention",
    )(count, queries, own, core, y, bias, part, stat)


def masks(rows, count, plen):
    owned, maxp, per_pass = rows.shape
    selected = maxp * per_pass
    touched = jnp.any(rows[..., None] == jnp.arange(plen, dtype=jnp.int32), axis=2)
    touched = touched.reshape(owned, 1, maxp * plen)
    key_pos = jnp.arange(maxp * plen, dtype=jnp.int32)
    slot = jnp.arange(selected, dtype=jnp.int32) // per_pass
    query_pos = slot * plen + rows.reshape(owned, selected)
    seen = (key_pos // plen < count[:, None, None]) & (key_pos <= query_pos[:, :, None])
    cached_bias = jnp.where(seen & ~touched, 0.0, HIDDEN).astype(jnp.float32)
    seen = (slot < count[:, None, None]) & (query_pos[:, None, :] <= query_pos[:, :, None])
    fresh_bias = jnp.where(seen, 0.0, HIDDEN).astype(jnp.float32)
    return cached_bias, fresh_bias


def ring_projection(rows_in, norm_gain, kv_weight):
    shards = lax.axis_size("store")
    me = lax.axis_index("store")
    side = lax.axis_index("parts")
    ring = shards // GROUP
    z, member = me // GROUP, me % GROUP
    owned, selected, width = rows_in.shape
    depth, features = kv_weight.shape
    half = depth // 2

    mine = lax.dynamic_slice_in_dim(kv_weight, side * half, half, 0)
    below = send(mine, 1)
    above = send(mine, -1)
    low = send(below[: half // 2], 1)
    high = send(above[half // 2 :], -1)

    steps = jnp.array([0, 0, -1, -1, 1, 1, 2, 2], jnp.int32)
    blocks = (z + steps) % ring
    halves = jnp.array([0, 1, 0, 1, 0, 1, 0, 1], jnp.int32)
    halves = jnp.where(steps == 0, halves, halves ^ side)
    targets = member ^ jnp.arange(GROUP, dtype=jnp.int32)
    offs = (blocks[None] * GROUP + targets[:, None]) * depth + halves[None] * half
    offs = (offs // 128).reshape(-1)
    flat = rows_in.reshape(owned * selected, width)
    acts = norm_rows(flat, norm_gain, offs, half)
    acts = [acts[0]] + [flip(acts[j], j) for j in (1, 2, 3)]

    acc = first_part(acts, [kv_weight, below, swap(below), above, swap(above)])
    keep, out = second_part(acts, [low, high, swap(low), swap(high)], acc)
    count = owned * selected
    back = flip(out, 1)
    y_out = (keep[count:] + back[count:].astype(jnp.float32)).astype(jnp.bfloat16)
    return keep[:count], back[:count], flip(y_out, 2)


def gathered_projection(rows_in, norm_gain, kv_weight):
    owned, selected, width = rows_in.shape
    wide = rows_in.reshape(owned * selected, width).astype(jnp.float32)
    inv = lax.rsqrt(jnp.mean(wide * wide, axis=-1, keepdims=True) + 1e-05)
    normed = (wide * inv * norm_gain.astype(jnp.float32)).astype(jnp.bfloat16)
    fresh = dot(normed, lax.all_gather(kv_weight, "store", axis=0, tiled=True))
    none = jnp.zeros(fresh.shape, jnp.bfloat16)
    return fresh, none, none


def ring_pages(store_pages, passage_home, passage_ids):
    shards = lax.axis_size("store")
    me = lax.axis_index("store")
    ring = shards // GROUP
    z, member = me // GROUP, me % GROUP
    local, plen, _, kvw = store_pages.shape
    own = store_pages.reshape(local * plen, 2 * kvw)
    mid = local * plen // 2
    below = send(own, 1)
    above = send(own, -1)
    low = send(below[:mid], 1)
    high = send(above[mid:], -1)
    column = jnp.concatenate([own, below, above, low, high], axis=0)
    near = jnp.concatenate([column, flip(column, 2)], axis=0)
    far = flip(near, 1)
    owned = passage_ids.shape[0] // shards
    ids = lax.dynamic_slice_in_dim(passage_ids, me * owned, owned, 0)
    device = jnp.arange(shards, dtype=jnp.int32)
    apart = (device // GROUP - z) % ring
    rank = jnp.where(apart == 0, 0, jnp.where(apart == ring - 1, 1, apart + 1))
    rel = (device % GROUP) ^ member
    place = ((rel % 2) * 2 + rel // 2) * ring + rank
    return place, passage_home, ids, near, far


def sent_pages(store_pages, passage_home, passage_ids):
    shards = lax.axis_size("store")
    me = lax.axis_index("store")
    local, plen, _, kvw = store_pages.shape
    owned = passage_ids.shape[0] // shards
    positions = owned * passage_ids.shape[1]
    cap = (positions + shards - 1) // shards
    slots = passage_home[passage_ids]
    home_shard = (slots // local).reshape(shards, positions)
    local_slot = (slots % local).reshape(shards, positions)
    earlier = jnp.tril(jnp.ones((positions, positions), jnp.bool_), -1)
    same = home_shard[:, :, None] == home_shard[:, None, :]
    rank = jnp.sum(same & earlier[None], axis=2)
    ladder = jnp.arange(cap, dtype=jnp.int32)
    hit = (home_shard[:, :, None] == me) & (rank[:, :, None] == ladder[None, None, :])
    pick = jnp.sum(jnp.where(hit, local_slot[:, :, None], 0), axis=1)
    outgoing = store_pages[pick.reshape(shards * cap)]
    my_shard = lax.dynamic_slice_in_dim(home_shard, me, 1, 0)[0]
    my_rank = lax.dynamic_slice_in_dim(rank, me, 1, 0)[0]
    arrived = lax.all_to_all(outgoing, "store", split_axis=0, concat_axis=0, tiled=True)
    arrived = arrived.reshape(shards * cap * plen, 2 * kvw)
    middle = arrived.shape[0] // 2
    place = jnp.arange(shards * cap, dtype=jnp.int32)
    home = (my_shard * cap + my_rank).astype(jnp.int32)
    ids = jnp.arange(positions, dtype=jnp.int32).reshape(owned, passage_ids.shape[1])
    return place, home, ids, arrived[:middle], arrived[middle:]


def per_device(
    rows_in,
    norm_gain,
    kv_weight,
    queries,
    store_pages,
    passage_home,
    passage_ids,
    passage_count,
    recompute_rows,
):
    shards = lax.axis_size("store")
    me = lax.axis_index("store")
    owned, selected, _ = rows_in.shape
    local, plen = store_pages.shape[:2]
    ringed = shards == 4 * GROUP and lax.axis_size("parts") == 2 and kv_weight.shape[0] % 512 == 0
    if ringed and local % 2 == 0:
        pages = ring_pages(store_pages, passage_home, passage_ids)
        per_dev = local
    else:
        pages = sent_pages(store_pages, passage_home, passage_ids)
        per_dev = 1
    rows = lax.dynamic_slice_in_dim(recompute_rows, me * owned, owned, 0)
    cached_bias, fresh_bias = masks(rows, passage_count, plen)
    part, stat = cached_attention(per_dev, *pages, queries, cached_bias)
    project = ring_projection if ringed else gathered_projection
    terms = project(rows_in, norm_gain, kv_weight)
    terms = [t.reshape(owned, selected, t.shape[1]) for t in terms]
    return fresh_attention(passage_ids.shape[1], passage_count, queries, *terms, fresh_bias, part, stat)


def solution(mesh):
    in_specs = (
        P(("parts", "store"), None, None),
        P(),
        P("store", None),
        P(("parts", "store"), None, None),
        P(("parts", "store"), None, None, None),
        P("parts"),
        P("parts", None),
        P(("parts", "store")),
        P("parts", None, None),
    )
    out_specs = P(("parts", "store"), None, None)
    return jax.shard_map(
        per_device, mesh=mesh, in_specs=in_specs, out_specs=out_specs, check_vma=False
    )
```

```python
import functools
import math

import jax
import jax.numpy as jnp
from jax import lax
from jax.experimental import pallas as pl
from jax.experimental.pallas import tpu as pltpu
from jax.sharding import PartitionSpec as P

QUERY_HEADS = 32
KEY_VALUE_HEADS = 4
HEAD_SIZE = 128
HEAD_GROUP = QUERY_HEADS // KEY_VALUE_HEADS
GROUP = 4
HIDDEN = -1e30
EXP2_SCALE = math.log2(math.e) / math.sqrt(HEAD_SIZE)
VMEM_LIMIT = 48 * 2**20


def params(**more):
    return pltpu.CompilerParams(vmem_limit_bytes=VMEM_LIMIT, **more)


def whole():
    return pl.BlockSpec(memory_space=pltpu.VMEM)


def smem():
    return pl.BlockSpec(memory_space=pltpu.SMEM)


def send(x, steps):
    shards = lax.axis_size("store")
    pairs = [(i, (i + steps * GROUP) % shards) for i in range(shards)]
    return lax.ppermute(x, "store", pairs)


def flip(x, bits):
    pairs = [(i, i ^ bits) for i in range(lax.axis_size("store"))]
    return lax.ppermute(x, "store", pairs)


def swap(x):
    return lax.ppermute(x, "parts", [(0, 1), (1, 0)])


def norm_kernel(chunk, chunks, offs_ref, rows_ref, gain_ref, own_ref, y_ref, core_ref, held):
    wide = rows_ref[...].astype(jnp.float32)
    inv = lax.rsqrt(jnp.mean(wide * wide, axis=-1, keepdims=True) + 1e-05)
    held[...] = (wide * inv * gain_ref[...].astype(jnp.float32)).astype(jnp.bfloat16)
    for j in range(GROUP):
        for k in range(chunks):
            at = pl.multiple_of(offs_ref[j * chunks + k] * 128, 128)
            piece = held[:, pl.ds(at, chunk)]
            if j < 2:
                out = (own_ref, core_ref)[j]
                out[:, k * chunk : (k + 1) * chunk] = piece
            else:
                y_ref[j - 2, :, k * chunk : (k + 1) * chunk] = piece


def norm_rows(rows, gain, offs, chunk):
    count, width = rows.shape
    chunks = width // GROUP // chunk
    block = 32
    depth = width // GROUP
    one = jax.ShapeDtypeStruct((count, depth), jnp.bfloat16)
    two = jax.ShapeDtypeStruct((2, count, depth), jnp.bfloat16)
    one_spec = pl.BlockSpec((block, depth), lambda i: (i, 0))
    own, y, core = pl.pallas_call(
        functools.partial(norm_kernel, chunk, chunks),
        out_shape=[one, two, one],
        grid=(count // block,),
        in_specs=[
            smem(),
            pl.BlockSpec((block, width), lambda i: (i, 0)),
            pl.BlockSpec((1, width), lambda i: (0, 0)),
        ],
        out_specs=[one_spec, pl.BlockSpec((2, block, depth), lambda i: (0, i, 0)), one_spec],
        scratch_shapes=[pltpu.VMEM((block, width), jnp.bfloat16)],
        compiler_params=params(),
        cost_estimate=pl.CostEstimate(
            flops=6 * count * width, bytes_accessed=4 * count * width, transcendentals=0
        ),
        name="norm",
    )(offs, rows, gain.reshape(1, width))
    return own, y.reshape(2 * count, depth), core


def dot(a, b):
    return jnp.dot(a, b, preferred_element_type=jnp.float32)


def project_kernel(a0, a1, a2, a3, *refs):
    weights, (keep, send) = refs[:-2], refs[-2:]
    rows = a0.shape[0]
    for j, a in enumerate((a0, a1, a2, a3)):
        total = None
        at = 0
        for w in weights:
            depth = w.shape[0]
            term = dot(a[:, at : at + depth], w[...])
            total = term if total is None else total + term
            at += depth
        place = slice((j // 2) * rows, (j // 2 + 1) * rows)
        if j % 2:
            send[place, :] = total.astype(jnp.bfloat16)
        else:
            keep[place, :] = total


def project(acts, own, first, weights, half):
    rows, depth = acts[0].shape
    features = weights[0].shape[1]
    block = 256
    shift = first * features // block
    return pl.pallas_call(
        project_kernel,
        out_shape=[
            jax.ShapeDtypeStruct((2 * rows, features), jnp.float32),
            jax.ShapeDtypeStruct((2 * rows, features), jnp.bfloat16),
        ],
        grid=(features // block,),
        in_specs=[pl.BlockSpec((rows, depth), lambda i: (0, 0))] * GROUP
        + [pl.BlockSpec((own.shape[0], block), lambda i: (0, i + shift))]
        + [pl.BlockSpec((half, block), lambda i: (0, i)) for w in weights],
        out_specs=[pl.BlockSpec((2 * rows, block), lambda i: (0, i))] * 2,
        compiler_params=params(),
        cost_estimate=pl.CostEstimate(
            flops=2 * GROUP * rows * depth * features,
            bytes_accessed=2 * depth * (GROUP * rows + features) + 6 * GROUP * rows * features,
            transcendentals=0,
        ),
        name="project",
    )(*acts, own, *weights)


def stacked_queries(q_ref, head):
    parts = []
    for i in range(HEAD_GROUP):
        at = (head * HEAD_GROUP + i) * HEAD_SIZE
        parts.append(q_ref[0, :, at : at + HEAD_SIZE].astype(jnp.float32))
    return jnp.concatenate(parts, axis=0).astype(jnp.bfloat16)


def scores_of(q, keys, bias):
    s = lax.dot_general(q, keys, (((1,), (1,)), ((), ())), preferred_element_type=jnp.float32)
    rows, cols = bias.shape
    s = (s * EXP2_SCALE).reshape(HEAD_GROUP, rows, cols) + bias[None]
    return s.reshape(HEAD_GROUP * rows, cols)


def cached_kernel(per_dev, place_ref, home_ref, ids_ref, q_ref, *refs):
    sources, (bias_ref, out_ref, stat_ref, pages, context, sems) = refs[:-6], refs[-6:]
    r = pl.program_id(0)
    maxp = ids_ref.shape[1]
    plen = context.shape[1] // maxp

    @pl.when(r == 0)
    def _():
        copies = []
        at = 0
        for n, source in enumerate(sources):
            rows = source.shape[0]
            copies.append(pltpu.make_async_copy(source, pages.at[pl.ds(at, rows)], sems.at[n]))
            at += rows
        for copy in copies:
            copy.start()
        for copy in copies:
            copy.wait()

    for m in range(maxp):
        slot = home_ref[ids_ref[r, m]]
        block = place_ref[slot // per_dev] * (2 * per_dev) + slot % per_dev
        for c in range(2):
            at = pl.multiple_of((block + c * per_dev) * plen, plen)
            context[c, m * plen : (m + 1) * plen, :] = pages[pl.ds(at, plen), :]
    bias = bias_ref[0]
    lane = lax.broadcasted_iota(jnp.int32, (HEAD_GROUP * bias.shape[0], HEAD_SIZE), 1)
    for g in range(KEY_VALUE_HEADS):
        q = stacked_queries(q_ref, g)
        keys = context[0, :, g * HEAD_SIZE : (g + 1) * HEAD_SIZE]
        values = context[1, :, g * HEAD_SIZE : (g + 1) * HEAD_SIZE]
        s = scores_of(q, keys, bias)
        top = jnp.max(s, axis=-1, keepdims=True)
        e = jnp.exp2(s - top)
        total = jnp.sum(e, axis=-1, keepdims=True)
        out_ref[0, g] = dot(e.astype(jnp.bfloat16), values)
        stat_ref[0, g] = jnp.where(lane < HEAD_SIZE // 2, top, total)


def cached_attention(per_dev, place, home, ids, sources, queries, bias):
    owned, rows, width = queries.shape
    context = bias.shape[2]
    features = sources[0].shape[1]
    stacked = HEAD_GROUP * rows
    state = jax.ShapeDtypeStruct((owned, KEY_VALUE_HEADS, stacked, HEAD_SIZE), jnp.float32)
    state_spec = pl.BlockSpec((1, KEY_VALUE_HEADS, stacked, HEAD_SIZE), lambda r: (r, 0, 0, 0))
    return pl.pallas_call(
        functools.partial(cached_kernel, per_dev),
        out_shape=[state, state],
        grid=(owned,),
        in_specs=[
            smem(),
            smem(),
            smem(),
            pl.BlockSpec((1, rows, width), lambda r: (r, 0, 0)),
            *[pl.BlockSpec(memory_space=pl.ANY)] * len(sources),
            pl.BlockSpec((1, rows, context), lambda r: (r, 0, 0)),
        ],
        out_specs=[state_spec, state_spec],
        scratch_shapes=[
            pltpu.VMEM((sum(x.shape[0] for x in sources), features), jnp.bfloat16),
            pltpu.VMEM((2, context, features), jnp.bfloat16),
            pltpu.SemaphoreType.DMA((len(sources),)),
        ],
        compiler_params=params(),
        cost_estimate=pl.CostEstimate(
            flops=4 * owned * rows * width * context,
            bytes_accessed=8 * sources[0].size + 2 * queries.size + 8 * owned * stacked * 4 * HEAD_SIZE,
            transcendentals=owned * rows * QUERY_HEADS * context,
        ),
        name="cached_attention",
    )(place, home, ids, queries, *sources, bias)


def added(own_ref, core_ref, y_ref):
    total = own_ref[0] + core_ref[0].astype(jnp.float32) + y_ref[0].astype(jnp.float32)
    return total.astype(jnp.bfloat16)


def fresh_kernel(
    maxp, count_ref, q_ref, ko_ref, kc_ref, ky_ref, vo_ref, vc_ref, vy_ref, bias_ref, part_ref,
    stat_ref, out_ref,
):
    r = pl.program_id(0)
    fresh_keys = added(ko_ref, kc_ref, ky_ref)
    fresh_values = added(vo_ref, vc_ref, vy_ref)
    bias = bias_ref[0]
    rows = bias.shape[0]
    per_pass = rows // maxp
    slot = lax.broadcasted_iota(jnp.int32, (rows, HEAD_SIZE), 0) // per_pass
    live = slot < count_ref[r]
    for g in range(KEY_VALUE_HEADS):
        q = stacked_queries(q_ref, g)
        keys = fresh_keys[:, g * HEAD_SIZE : (g + 1) * HEAD_SIZE]
        values = fresh_values[:, g * HEAD_SIZE : (g + 1) * HEAD_SIZE]
        s = scores_of(q, keys, bias)
        top1 = stat_ref[0, g, :, 0:1]
        sum1 = stat_ref[0, g, :, HEAD_SIZE // 2 : HEAD_SIZE // 2 + 1]
        top = jnp.maximum(top1, jnp.max(s, axis=-1, keepdims=True))
        e = jnp.exp2(s - top)
        keep = jnp.exp2(top1 - top)
        inv = 1.0 / (sum1 * keep + jnp.sum(e, axis=-1, keepdims=True))
        result = (part_ref[0, g] * keep + dot(e.astype(jnp.bfloat16), values)) * inv
        for i in range(HEAD_GROUP):
            at = (g * HEAD_GROUP + i) * HEAD_SIZE
            one = result[i * rows : (i + 1) * rows]
            out_ref[0, :, at : at + HEAD_SIZE] = jnp.where(live, one, 0.0).astype(jnp.bfloat16)


def fresh_attention(maxp, count, queries, terms, bias, part, stat):
    owned, rows, width = queries.shape
    features = terms[0].shape[-1]
    stacked = HEAD_GROUP * rows
    state_spec = pl.BlockSpec((1, KEY_VALUE_HEADS, stacked, HEAD_SIZE), lambda r: (r, 0, 0, 0))
    row_spec = pl.BlockSpec((1, rows, features), lambda r: (r, 0, 0))
    query_spec = pl.BlockSpec((1, rows, width), lambda r: (r, 0, 0))
    return pl.pallas_call(
        functools.partial(fresh_kernel, maxp),
        out_shape=jax.ShapeDtypeStruct(queries.shape, jnp.bfloat16),
        grid=(owned,),
        in_specs=[
            smem(),
            query_spec,
            *[row_spec] * 6,
            pl.BlockSpec((1, rows, rows), lambda r: (r, 0, 0)),
            state_spec,
            state_spec,
        ],
        out_specs=query_spec,
        compiler_params=params(),
        cost_estimate=pl.CostEstimate(
            flops=4 * owned * rows * width * rows,
            bytes_accessed=4 * queries.size + 8 * part.size,
            transcendentals=owned * rows * QUERY_HEADS * rows,
        ),
        name="fresh_attention",
    )(count, queries, *terms, bias, part, stat)


def masks(rows, count, plen):
    owned, maxp, per_pass = rows.shape
    selected = maxp * per_pass
    touched = jnp.any(rows[..., None] == jnp.arange(plen, dtype=jnp.int32), axis=2)
    touched = touched.reshape(owned, 1, maxp * plen)
    key_pos = jnp.arange(maxp * plen, dtype=jnp.int32)
    slot = jnp.arange(selected, dtype=jnp.int32) // per_pass
    query_pos = slot * plen + rows.reshape(owned, selected)
    seen = (key_pos // plen < count[:, None, None]) & (key_pos <= query_pos[:, :, None])
    cached_bias = jnp.where(seen & ~touched, 0.0, HIDDEN).astype(jnp.float32)
    seen = (slot < count[:, None, None]) & (query_pos[:, None, :] <= query_pos[:, :, None])
    fresh_bias = jnp.where(seen, 0.0, HIDDEN).astype(jnp.float32)
    return cached_bias, fresh_bias


def after(x, *earlier):
    return lax.optimization_barrier((x, *earlier))[0]


def ring_plan(rows_in, norm_gain, kv_weight, store_pages):
    shards = lax.axis_size("store")
    me = lax.axis_index("store")
    side = lax.axis_index("parts")
    ring = shards // GROUP
    z, member = me // GROUP, me % GROUP
    owned, selected, width = rows_in.shape
    depth, features = kv_weight.shape
    local, plen, _, kvw = store_pages.shape
    half = depth // 2
    columns = features // 2

    pages = store_pages.reshape(local * plen, 2, kvw)
    mine = [
        lax.dynamic_slice(kv_weight, (side * half, n * columns), (half, columns)) for n in range(2)
    ]
    own = jnp.concatenate([pages[:, 0], pages[:, 1]], axis=0)
    a0 = jnp.concatenate([mine[0], own], axis=0)
    a1, b1 = send(a0, 1), send(mine[1], 1)
    gate = a0

    steps = jnp.arange(2 * ring, dtype=jnp.int32) // 2
    blocks = (z - steps) % ring
    halves = jnp.arange(2 * ring, dtype=jnp.int32) % 2
    halves = jnp.where(steps == 0, halves, halves ^ side)
    targets = member ^ jnp.arange(GROUP, dtype=jnp.int32)
    offs = (blocks[None] * GROUP + targets[:, None]) * depth + halves[None] * half
    offs = (offs // 128).reshape(-1)
    flat = rows_in.reshape(owned * selected, width)
    acts = norm_rows(flat, norm_gain, after(offs, gate), half)
    y_acts = flip(acts[1], 2)
    near_act = flip(acts[2], 1)

    a2 = send(after(a1, near_act), 1)
    xa1 = swap(after(a1[:half], near_act))
    b2 = send(after(b1, near_act), 1)
    xb1 = swap(b1)
    a3 = send(after(a2, xa1), 1)
    xa2 = swap(after(a2[:half], xa1))
    b3 = send(after(b2, xb1), 1)
    xb2 = swap(after(b2, xb1))
    xa3 = swap(after(a3[:half], xa2))
    column = jnp.concatenate([own, a1[half:], a2[half:], a3[half:]], axis=0)
    column = after(column, y_acts)
    y_column = flip(column, 2)
    y_far = flip(y_acts[acts[0].shape[0] :], 1)
    xb3 = swap(after(b3, xb2))
    far = flip(column, 1)
    y_column_far = flip(y_column, 1)
    acts = [acts[0], near_act, y_acts, y_far]
    chunks = [[a1, xa1, a2, xa2, a3, xa3], [b1, xb1, b2, xb2, b3, xb3]]

    count = owned * selected
    terms = []
    for n in range(2):
        keep, out = project(acts, kv_weight, n, chunks[n], half)
        back = flip(out, 1)
        y_out = (keep[count:] + back[count:].astype(jnp.float32)).astype(jnp.bfloat16)
        terms.append((keep[:count], back[:count], flip(y_out, 2)))

    device = jnp.arange(shards, dtype=jnp.int32)
    rank = (z - device // GROUP) % ring
    rel = (device % GROUP) ^ member
    place = ((rel % 2) * 2 + rel // 2) * ring + rank
    return (place, [column, y_column, far, y_column_far]), terms


def gathered_projection(rows_in, norm_gain, kv_weight):
    owned, selected, width = rows_in.shape
    wide = rows_in.reshape(owned * selected, width).astype(jnp.float32)
    inv = lax.rsqrt(jnp.mean(wide * wide, axis=-1, keepdims=True) + 1e-05)
    normed = (wide * inv * norm_gain.astype(jnp.float32)).astype(jnp.bfloat16)
    fresh = dot(normed, lax.all_gather(kv_weight, "store", axis=0, tiled=True))
    none = jnp.zeros((fresh.shape[0], fresh.shape[1] // 2), jnp.bfloat16)
    return [(part, none, none) for part in jnp.split(fresh, 2, axis=1)]


def sent_pages(store_pages, passage_home, passage_ids):
    shards = lax.axis_size("store")
    me = lax.axis_index("store")
    local, plen, _, kvw = store_pages.shape
    owned = passage_ids.shape[0] // shards
    positions = owned * passage_ids.shape[1]
    cap = (positions + shards - 1) // shards
    slots = passage_home[passage_ids]
    home_shard = (slots // local).reshape(shards, positions)
    local_slot = (slots % local).reshape(shards, positions)
    earlier = jnp.tril(jnp.ones((positions, positions), jnp.bool_), -1)
    same = home_shard[:, :, None] == home_shard[:, None, :]
    rank = jnp.sum(same & earlier[None], axis=2)
    ladder = jnp.arange(cap, dtype=jnp.int32)
    hit = (home_shard[:, :, None] == me) & (rank[:, :, None] == ladder[None, None, :])
    pick = jnp.sum(jnp.where(hit, local_slot[:, :, None], 0), axis=1)
    outgoing = store_pages[pick.reshape(shards * cap)]
    my_shard = lax.dynamic_slice_in_dim(home_shard, me, 1, 0)[0]
    my_rank = lax.dynamic_slice_in_dim(rank, me, 1, 0)[0]
    arrived = lax.all_to_all(outgoing, "store", split_axis=0, concat_axis=0, tiled=True)
    arrived = arrived.transpose(0, 2, 1, 3).reshape(shards * cap * 2 * plen, kvw)
    place = jnp.arange(shards * cap, dtype=jnp.int32)
    home = (my_shard * cap + my_rank).astype(jnp.int32)
    ids = jnp.arange(positions, dtype=jnp.int32).reshape(owned, passage_ids.shape[1])
    return place, home, ids, [arrived]


def per_device(
    rows_in,
    norm_gain,
    kv_weight,
    queries,
    store_pages,
    passage_home,
    passage_ids,
    passage_count,
    recompute_rows,
):
    shards = lax.axis_size("store")
    me = lax.axis_index("store")
    owned, selected, _ = rows_in.shape
    local, plen = store_pages.shape[:2]
    ringed = shards == 4 * GROUP and lax.axis_size("parts") == 2 and kv_weight.shape[0] % 512 == 0
    if ringed:
        (place, sources), terms = ring_plan(rows_in, norm_gain, kv_weight, store_pages)
        ids = lax.dynamic_slice_in_dim(passage_ids, me * owned, owned, 0)
        pages = (place, passage_home, ids, sources)
        per_dev = local
    else:
        terms = gathered_projection(rows_in, norm_gain, kv_weight)
        pages = sent_pages(store_pages, passage_home, passage_ids)
        per_dev = 1
    rows = lax.dynamic_slice_in_dim(recompute_rows, me * owned, owned, 0)
    cached_bias, fresh_bias = masks(rows, passage_count, plen)
    part, stat = cached_attention(per_dev, *pages, queries, cached_bias)
    terms = [t.reshape(owned, selected, t.shape[1]) for chunk in terms for t in chunk]
    return fresh_attention(passage_ids.shape[1], passage_count, queries, terms, fresh_bias, part, stat)


def solution(mesh):
    in_specs = (
        P(("parts", "store"), None, None),
        P(),
        P("store", None),
        P(("parts", "store"), None, None),
        P(("parts", "store"), None, None, None),
        P("parts"),
        P("parts", None),
        P(("parts", "store")),
        P("parts", None, None),
    )
    out_specs = P(("parts", "store"), None, None)
    return jax.shard_map(
        per_device, mesh=mesh, in_specs=in_specs, out_specs=out_specs, check_vma=False
    )
```

```python
import functools
import math

import jax
import jax.numpy as jnp
from jax import lax
from jax.experimental import pallas as pl
from jax.experimental.pallas import tpu as pltpu
from jax.sharding import PartitionSpec as P

QUERY_HEADS = 32
KEY_VALUE_HEADS = 4
HEAD_SIZE = 128
HEAD_GROUP = QUERY_HEADS // KEY_VALUE_HEADS
GROUP = 4
HIDDEN = -1e30
NEVER = 1 << 30
EXP2_SCALE = math.log2(math.e) / math.sqrt(HEAD_SIZE)
VMEM_LIMIT = 16 * 2**20


def params(**more):
    return pltpu.CompilerParams(vmem_limit_bytes=VMEM_LIMIT, **more)


def whole():
    return pl.BlockSpec(memory_space=pltpu.VMEM)


def smem():
    return pl.BlockSpec(memory_space=pltpu.SMEM)


def send(x, steps):
    shards = lax.axis_size("store")
    pairs = [(i, (i + steps * GROUP) % shards) for i in range(shards)]
    return lax.ppermute(x, "store", pairs)


def flip(x, bits):
    pairs = [(i, i ^ bits) for i in range(lax.axis_size("store"))]
    return lax.ppermute(x, "store", pairs)


def swap(x):
    return lax.ppermute(x, "parts", [(0, 1), (1, 0)])


def norm_kernel(chunk, chunks, offs_ref, rows_ref, gain_ref, own_ref, y_ref, core_ref, held):
    wide = rows_ref[...].astype(jnp.float32)
    inv = lax.rsqrt(jnp.mean(wide * wide, axis=-1, keepdims=True) + 1e-05)
    held[...] = (wide * inv * gain_ref[...].astype(jnp.float32)).astype(jnp.bfloat16)
    for j in range(GROUP):
        for k in range(chunks):
            at = pl.multiple_of(offs_ref[j * chunks + k] * 128, 128)
            piece = held[:, pl.ds(at, chunk)]
            if j < 2:
                out = (own_ref, core_ref)[j]
                out[:, k * chunk : (k + 1) * chunk] = piece
            else:
                y_ref[j - 2, :, k * chunk : (k + 1) * chunk] = piece


def norm_rows(rows, gain, offs, chunk):
    count, width = rows.shape
    chunks = width // GROUP // chunk
    block = 32
    depth = width // GROUP
    one = jax.ShapeDtypeStruct((count, depth), jnp.bfloat16)
    two = jax.ShapeDtypeStruct((2, count, depth), jnp.bfloat16)
    one_spec = pl.BlockSpec((block, depth), lambda i: (i, 0))
    own, y, core = pl.pallas_call(
        functools.partial(norm_kernel, chunk, chunks),
        out_shape=[one, two, one],
        grid=(count // block,),
        in_specs=[
            smem(),
            pl.BlockSpec((block, width), lambda i: (i, 0)),
            pl.BlockSpec((1, width), lambda i: (0, 0)),
        ],
        out_specs=[one_spec, pl.BlockSpec((2, block, depth), lambda i: (0, i, 0)), one_spec],
        scratch_shapes=[pltpu.VMEM((block, width), jnp.bfloat16)],
        compiler_params=params(),
        cost_estimate=pl.CostEstimate(
            flops=6 * count * width, bytes_accessed=4 * count * width, transcendentals=0
        ),
        name="norm",
    )(offs, rows, gain.reshape(1, width))
    return own, y.reshape(2 * count, depth), core


def dot(a, b):
    return jnp.dot(a, b, preferred_element_type=jnp.float32)


def project_kernel(a0, a1, a2, a3, *refs):
    weights, (keep, send) = refs[:-2], refs[-2:]
    rows = a0.shape[0]
    for j, a in enumerate((a0, a1, a2, a3)):
        total = None
        at = 0
        for w in weights:
            depth = w.shape[0]
            term = dot(a[:, at : at + depth], w[...])
            total = term if total is None else total + term
            at += depth
        place = slice((j // 2) * rows, (j // 2 + 1) * rows)
        if j % 2:
            send[place, :] = total.astype(jnp.bfloat16)
        else:
            keep[place, :] = total


def project(acts, own, first, weights, half):
    rows, depth = acts[0].shape
    features = weights[0].shape[1]
    block = 256
    shift = first * features // block
    return pl.pallas_call(
        project_kernel,
        out_shape=[
            jax.ShapeDtypeStruct((2 * rows, features), jnp.float32),
            jax.ShapeDtypeStruct((2 * rows, features), jnp.bfloat16),
        ],
        grid=(features // block,),
        in_specs=[pl.BlockSpec((rows, depth), lambda i: (0, 0))] * GROUP
        + [pl.BlockSpec((own.shape[0], block), lambda i: (0, i + shift))]
        + [pl.BlockSpec((half, block), lambda i: (0, i)) for w in weights],
        out_specs=[pl.BlockSpec((2 * rows, block), lambda i: (0, i))] * 2,
        compiler_params=params(),
        cost_estimate=pl.CostEstimate(
            flops=2 * GROUP * rows * depth * features,
            bytes_accessed=2 * depth * (GROUP * rows + features) + 6 * GROUP * rows * features,
            transcendentals=0,
        ),
        name="project",
    )(*acts, own, *weights)


def by_request(*shape):
    return pl.BlockSpec((1, *shape), lambda r: (r,) + (0,) * len(shape))


def against(a, b, dims):
    return lax.dot_general(a, b, (dims, ((), ())), preferred_element_type=jnp.float32)

def stacked_queries(q_ref, group):
    heads = []
    for i in range(HEAD_GROUP):
        at = (group * HEAD_GROUP + i) * HEAD_SIZE
        heads.append(q_ref[0, :, at : at + HEAD_SIZE].astype(jnp.float32))
    return jnp.concatenate(heads, axis=0).astype(jnp.bfloat16)


def cached_kernel(per_dev, place_ref, home_ref, ids_ref, rows_ref, count_ref, q_ref, *refs):
    sources, (query_pos_ref, out_ref, stat_ref, stacked_ref, pages, context, bias, sems) = refs[:-8], refs[-8:]
    r = pl.program_id(0)
    maxp = ids_ref.shape[1]
    plen = context.shape[1] // maxp

    @pl.when(r == 0)
    def _():
        copies = []
        at = 0
        for n, source in enumerate(sources):
            rows = source.shape[0]
            copies.append(pltpu.make_async_copy(source, pages.at[pl.ds(at, rows)], sems.at[n]))
            at += rows
        for copy in copies:
            copy.start()
        for copy in copies:
            copy.wait()

    for m in range(maxp):
        slot = home_ref[ids_ref[r, m]]
        block = place_ref[slot // per_dev] * (2 * per_dev) + slot % per_dev
        for c in range(2):
            at = pl.multiple_of((block + c * per_dev) * plen, plen)
            context[c, m * plen : (m + 1) * plen, :] = pages[pl.ds(at, plen), :]
    per_pass = rows_ref.shape[1] // maxp
    row = lax.broadcasted_iota(jnp.int32, (plen, bias.shape[1]), 0)
    for m in range(maxp):
        hidden = m >= count_ref[r]
        for i in range(per_pass):
            hidden = hidden | (row == rows_ref[r, m * per_pass + i])
        key_pos = jnp.where(hidden, NEVER, row + m * plen)
        bias[m * plen : (m + 1) * plen, :] = jnp.where(key_pos <= query_pos_ref[0], 0.0, HIDDEN)
    for g in range(KEY_VALUE_HEADS):
        keys = context[0, :, g * HEAD_SIZE : (g + 1) * HEAD_SIZE]
        values = context[1, :, g * HEAD_SIZE : (g + 1) * HEAD_SIZE]
        q = stacked_queries(q_ref, g)
        stacked_ref[0, g] = q
        s = against(keys, q, ((1,), (1,))) * EXP2_SCALE + bias[...]
        top = jnp.max(s, axis=0, keepdims=True)
        e = jnp.exp2(s - top)
        stat_ref[0, g, 0:1] = top
        stat_ref[0, g, 1:2] = jnp.sum(e, axis=0, keepdims=True)
        out_ref[0, g] = against(values, e.astype(jnp.bfloat16), ((0,), (0,)))


def cached_attention(per_dev, plen, place, home, ids, sources, rows, count, queries, query_pos):
    owned, selected, width = queries.shape
    stacked = HEAD_GROUP * selected
    context = ids.shape[1] * plen
    features = sources[0].shape[1]
    heads = KEY_VALUE_HEADS
    return pl.pallas_call(
        functools.partial(cached_kernel, per_dev),
        out_shape=[
            jax.ShapeDtypeStruct((owned, heads, HEAD_SIZE, stacked), jnp.float32),
            jax.ShapeDtypeStruct((owned, heads, 2, stacked), jnp.float32),
            jax.ShapeDtypeStruct((owned, heads, stacked, HEAD_SIZE), jnp.bfloat16),
        ],
        grid=(owned,),
        in_specs=[
            *[smem()] * 5,
            by_request(selected, width),
            *[pl.BlockSpec(memory_space=pl.ANY)] * len(sources),
            by_request(1, stacked),
        ],
        out_specs=[
            by_request(heads, HEAD_SIZE, stacked),
            by_request(heads, 2, stacked),
            by_request(heads, stacked, HEAD_SIZE),
        ],
        scratch_shapes=[
            pltpu.VMEM((sum(x.shape[0] for x in sources), features), jnp.bfloat16),
            pltpu.VMEM((2, context, features), jnp.bfloat16),
            pltpu.VMEM((context, stacked), jnp.float32),
            pltpu.SemaphoreType.DMA((len(sources),)),
        ],
        compiler_params=params(),
        cost_estimate=pl.CostEstimate(
            flops=4 * queries.size * context,
            bytes_accessed=4 * queries.size + 8 * sources[0].size,
            transcendentals=owned * heads * stacked * context,
        ),
        name="cached_attention",
    )(place, home, ids, rows, count, queries, *sources, query_pos)


def added(own_ref, *others):
    total = own_ref[0]
    for other in others:
        total = total + other[0].astype(jnp.float32)
    return total.astype(jnp.bfloat16)


def fresh_kernel(
    maxp, count_ref, q_ref, k0, k1, k2, v0, v1, v2, query_pos_ref, part_ref, stat_ref, out_ref,
):
    r = pl.program_id(0)
    fresh_keys = added(k0, k1, k2)
    fresh_values = added(v0, v1, v2)
    rows = fresh_keys.shape[0]
    per_pass = rows // maxp
    slot = lax.broadcasted_iota(jnp.int32, (rows, HEAD_SIZE), 0) // per_pass
    live = slot < count_ref[r]
    across = jnp.broadcast_to(query_pos_ref[0, :, :HEAD_SIZE], (HEAD_SIZE, HEAD_SIZE))
    key_pos = jnp.where(live, across.T[:rows], NEVER)[:, :1]
    bias = jnp.where(key_pos <= query_pos_ref[0], 0.0, HIDDEN)
    for g in range(KEY_VALUE_HEADS):
        keys = fresh_keys[:, g * HEAD_SIZE : (g + 1) * HEAD_SIZE]
        values = fresh_values[:, g * HEAD_SIZE : (g + 1) * HEAD_SIZE]
        s = against(keys, q_ref[0, g], ((1,), (1,))) * EXP2_SCALE + bias
        top1 = stat_ref[0, g, 0:1]
        top = jnp.maximum(top1, jnp.max(s, axis=0, keepdims=True))
        e = jnp.exp2(s - top)
        keep = jnp.exp2(top1 - top)
        inv = 1.0 / (stat_ref[0, g, 1:2] * keep + jnp.sum(e, axis=0, keepdims=True))
        term = against(values, e.astype(jnp.bfloat16), ((0,), (0,)))
        result = ((part_ref[0, g] * keep + term) * inv).T
        for i in range(HEAD_GROUP):
            at = (g * HEAD_GROUP + i) * HEAD_SIZE
            one = result[i * rows : (i + 1) * rows]
            out_ref[0, :, at : at + HEAD_SIZE] = jnp.where(live, one, 0.0).astype(jnp.bfloat16)


def fresh_attention(maxp, count, queries, terms, query_pos, part, stat):
    owned, heads, stacked, _ = queries.shape
    rows, features = terms[0].shape[1:]
    width = QUERY_HEADS * HEAD_SIZE
    return pl.pallas_call(
        functools.partial(fresh_kernel, maxp),
        out_shape=jax.ShapeDtypeStruct((owned, rows, width), jnp.bfloat16),
        grid=(owned,),
        in_specs=[
            smem(),
            by_request(heads, stacked, HEAD_SIZE),
            *[by_request(rows, features)] * 6,
            by_request(1, stacked),
            by_request(heads, HEAD_SIZE, stacked),
            by_request(heads, 2, stacked),
        ],
        out_specs=by_request(rows, width),
        compiler_params=params(),
        cost_estimate=pl.CostEstimate(
            flops=4 * queries.size * rows,
            bytes_accessed=8 * queries.size,
            transcendentals=owned * heads * stacked * rows,
        ),
        name="fresh_attention",
    )(count, queries, *terms, query_pos, part, stat)


def query_positions(rows, plen):
    owned, maxp, per_pass = rows.shape
    slot = jnp.arange(maxp * per_pass, dtype=jnp.int32) // per_pass
    at = slot * plen + rows.reshape(owned, maxp * per_pass)
    return jnp.tile(at, (1, HEAD_GROUP))[:, None, :]


def together(*arrays):
    return lax.optimization_barrier(arrays)


def after(x, *earlier):
    return lax.optimization_barrier((x, *earlier))[0]


def ring_plan(rows_in, norm_gain, kv_weight, store_pages, small):
    shards = lax.axis_size("store")
    me = lax.axis_index("store")
    side = lax.axis_index("parts")
    ring = shards // GROUP
    z, member = me // GROUP, me % GROUP
    owned, selected, width = rows_in.shape
    depth, features = kv_weight.shape
    local, plen, _, kvw = store_pages.shape
    half = depth // 2
    columns = features // 2
    count = owned * selected

    pages = store_pages.reshape(local * plen, 2, kvw)
    mine = [
        lax.dynamic_slice(kv_weight, (side * half, n * columns), (half, columns)) for n in range(2)
    ]
    own = jnp.concatenate([pages[:, 0], pages[:, 1]], axis=0)
    a0 = jnp.concatenate([mine[0], own], axis=0)
    a1 = send(a0, 1)
    b1 = send(mine[1], 1)

    steps = jnp.arange(2 * ring, dtype=jnp.int32) // 2
    blocks = (z - steps) % ring
    halves = jnp.arange(2 * ring, dtype=jnp.int32) % 2
    halves = jnp.where(steps == 0, halves, halves ^ side)
    targets = member ^ jnp.arange(GROUP, dtype=jnp.int32)
    offs = (blocks[None] * GROUP + targets[:, None]) * depth + halves[None] * half
    offs = (offs // 128).reshape(-1)

    device = jnp.arange(shards, dtype=jnp.int32)
    rank = (z - device // GROUP) % ring
    rel = (device % GROUP) ^ member
    place = ((rel % 2) * 2 + rel // 2) * ring + rank
    acts = norm_rows(rows_in.reshape(count, width), norm_gain, after(offs, a0), half)
    y_acts = flip(after(acts[1], b1), 2)
    near_act = flip(acts[2], 1)
    a1, near_act, place, *small = together(a1, near_act, place, *small)
    a2 = send(after(a1, b1), 1)
    xa1 = swap(after(a1[:half], near_act))
    b2 = send(after(b1, near_act), 1)
    xb1 = swap(b1)
    a3 = send(after(a2, xa1), 1)
    xa2 = swap(after(a2[:half], xa1))
    b3 = send(after(b2, xb1), 1)
    xb2 = swap(after(b2, xb1))
    y_far = flip(y_acts[count:], 1)
    xa3 = swap(after(a3[:half], xa2))
    xb3 = swap(after(b3, xb2))
    column = jnp.concatenate([own, a1[half:], a2[half:], a3[half:]], axis=0)
    y_column = flip(after(column, y_acts), 2)
    far = flip(after(column, b3), 1)
    y_column_far = flip(y_column, 1)
    acts = [acts[0], near_act, y_acts, y_far]

    chunks = [[a1, xa1, a2, xa2, a3, xa3], [b1, xb1, b2, xb2, b3, xb3]]
    terms = []
    for n in range(2):
        keep, out = project(acts, kv_weight, n, chunks[n], half)
        back = flip(out, 1)
        y_out = (keep[count:] + back[count:].astype(jnp.float32)).astype(jnp.bfloat16)
        terms += [keep[:count], back[:count], flip(y_out, 2)]
    return small, (place, [column, y_column, far, y_column_far]), terms


def gathered_projection(rows_in, norm_gain, kv_weight):
    owned, selected, width = rows_in.shape
    wide = rows_in.reshape(owned * selected, width).astype(jnp.float32)
    inv = lax.rsqrt(jnp.mean(wide * wide, axis=-1, keepdims=True) + 1e-05)
    normed = (wide * inv * norm_gain.astype(jnp.float32)).astype(jnp.bfloat16)
    fresh = dot(normed, lax.all_gather(kv_weight, "store", axis=0, tiled=True))
    none = jnp.zeros((fresh.shape[0], fresh.shape[1] // 2), jnp.bfloat16)
    keys, values = jnp.split(fresh, 2, axis=1)
    return [keys, none, none, values, none, none]


def sent_pages(store_pages, passage_home, passage_ids):
    shards = lax.axis_size("store")
    me = lax.axis_index("store")
    local, plen, _, kvw = store_pages.shape
    owned = passage_ids.shape[0] // shards
    positions = owned * passage_ids.shape[1]
    cap = (positions + shards - 1) // shards
    slots = passage_home[passage_ids]
    home_shard = (slots // local).reshape(shards, positions)
    local_slot = (slots % local).reshape(shards, positions)
    earlier = jnp.tril(jnp.ones((positions, positions), jnp.bool_), -1)
    same = home_shard[:, :, None] == home_shard[:, None, :]
    rank = jnp.sum(same & earlier[None], axis=2)
    ladder = jnp.arange(cap, dtype=jnp.int32)
    hit = (home_shard[:, :, None] == me) & (rank[:, :, None] == ladder[None, None, :])
    pick = jnp.sum(jnp.where(hit, local_slot[:, :, None], 0), axis=1)
    outgoing = store_pages[pick.reshape(shards * cap)]
    my_shard = lax.dynamic_slice_in_dim(home_shard, me, 1, 0)[0]
    my_rank = lax.dynamic_slice_in_dim(rank, me, 1, 0)[0]
    arrived = lax.all_to_all(outgoing, "store", split_axis=0, concat_axis=0, tiled=True)
    arrived = arrived.transpose(0, 2, 1, 3).reshape(shards * cap * 2 * plen, kvw)
    place = jnp.arange(shards * cap, dtype=jnp.int32)
    home = (my_shard * cap + my_rank).astype(jnp.int32)
    ids = jnp.arange(positions, dtype=jnp.int32).reshape(owned, passage_ids.shape[1])
    return place, home, ids, [arrived]


def per_device(
    rows_in,
    norm_gain,
    kv_weight,
    queries,
    store_pages,
    passage_home,
    passage_ids,
    passage_count,
    recompute_rows,
):
    shards = lax.axis_size("store")
    me = lax.axis_index("store")
    owned, selected, _ = rows_in.shape
    local, plen = store_pages.shape[:2]
    ringed = shards == 4 * GROUP and lax.axis_size("parts") == 2 and kv_weight.shape[0] % 512 == 0
    rows = lax.dynamic_slice_in_dim(recompute_rows, me * owned, owned, 0)
    query_pos = query_positions(rows, plen)
    flat_rows = rows.reshape(owned, selected)
    if ringed:
        ids = lax.dynamic_slice_in_dim(passage_ids, me * owned, owned, 0)
        small, (place, sources), terms = ring_plan(
            rows_in, norm_gain, kv_weight, store_pages, [ids, flat_rows, query_pos]
        )
        ids, flat_rows, query_pos = small
        pages = (place, passage_home, ids, sources)
        per_dev = local
    else:
        terms = gathered_projection(rows_in, norm_gain, kv_weight)
        pages = sent_pages(store_pages, passage_home, passage_ids)
        per_dev = 1
    part, stat, stacked = cached_attention(
        per_dev, plen, *pages, flat_rows, passage_count, queries, query_pos
    )
    terms = [t.reshape(owned, selected, t.shape[1]) for t in terms]
    maxp = passage_ids.shape[1]
    return fresh_attention(maxp, passage_count, stacked, terms, query_pos, part, stat)


def solution(mesh):
    in_specs = (
        P(("parts", "store"), None, None),
        P(),
        P("store", None),
        P(("parts", "store"), None, None),
        P(("parts", "store"), None, None, None),
        P("parts"),
        P("parts", None),
        P(("parts", "store")),
        P("parts", None, None),
    )
    out_specs = P(("parts", "store"), None, None)
    return jax.shard_map(
        per_device, mesh=mesh, in_specs=in_specs, out_specs=out_specs, check_vma=False
    )
```

```python
import functools
import math

import jax
import jax.numpy as jnp
from jax import lax
from jax.experimental import pallas as pl
from jax.experimental.pallas import tpu as pltpu
from jax.sharding import PartitionSpec as P

QUERY_HEADS = 32
KEY_VALUE_HEADS = 4
HEAD_SIZE = 128
HEAD_GROUP = QUERY_HEADS // KEY_VALUE_HEADS
GROUP = 4
HIDDEN = -1e30
NEVER = 1 << 30
EXP2_SCALE = math.log2(math.e) / math.sqrt(HEAD_SIZE)
VMEM_LIMIT = 16 * 2**20


def params(**more):
    return pltpu.CompilerParams(vmem_limit_bytes=VMEM_LIMIT, **more)


def whole():
    return pl.BlockSpec(memory_space=pltpu.VMEM)


def smem():
    return pl.BlockSpec(memory_space=pltpu.SMEM)


def send(x, steps):
    shards = lax.axis_size("store")
    pairs = [(i, (i + steps * GROUP) % shards) for i in range(shards)]
    return lax.ppermute(x, "store", pairs)


def flip(x, bits):
    pairs = [(i, i ^ bits) for i in range(lax.axis_size("store"))]
    return lax.ppermute(x, "store", pairs)


def swap(x):
    return lax.ppermute(x, "parts", [(0, 1), (1, 0)])


def norm_kernel(chunk, chunks, offs_ref, rows_ref, gain_ref, own_ref, y_ref, core_ref, held):
    wide = rows_ref[...].astype(jnp.float32)
    inv = lax.rsqrt(jnp.mean(wide * wide, axis=-1, keepdims=True) + 1e-05)
    held[...] = (wide * inv * gain_ref[...].astype(jnp.float32)).astype(jnp.bfloat16)
    for j in range(GROUP):
        for k in range(chunks):
            at = pl.multiple_of(offs_ref[j * chunks + k] * 128, 128)
            piece = held[:, pl.ds(at, chunk)]
            if j < 2:
                out = (own_ref, core_ref)[j]
                out[:, k * chunk : (k + 1) * chunk] = piece
            else:
                y_ref[j - 2, :, k * chunk : (k + 1) * chunk] = piece


def norm_rows(rows, gain, offs, chunk):
    count, width = rows.shape
    chunks = width // GROUP // chunk
    block = 32
    depth = width // GROUP
    one = jax.ShapeDtypeStruct((count, depth), jnp.bfloat16)
    two = jax.ShapeDtypeStruct((2, count, depth), jnp.bfloat16)
    one_spec = pl.BlockSpec((block, depth), lambda i: (i, 0))
    own, y, core = pl.pallas_call(
        functools.partial(norm_kernel, chunk, chunks),
        out_shape=[one, two, one],
        grid=(count // block,),
        in_specs=[
            smem(),
            pl.BlockSpec((block, width), lambda i: (i, 0)),
            pl.BlockSpec((1, width), lambda i: (0, 0)),
        ],
        out_specs=[one_spec, pl.BlockSpec((2, block, depth), lambda i: (0, i, 0)), one_spec],
        scratch_shapes=[pltpu.VMEM((block, width), jnp.bfloat16)],
        compiler_params=params(),
        cost_estimate=pl.CostEstimate(
            flops=6 * count * width, bytes_accessed=4 * count * width, transcendentals=0
        ),
        name="norm",
    )(offs, rows, gain.reshape(1, width))
    return own, y.reshape(2 * count, depth), core


def dot(a, b):
    return jnp.dot(a, b, preferred_element_type=jnp.float32)


def project_kernel(skip, shift, depths, begins, *refs):
    acts, refs = refs[:GROUP], refs[GROUP:]
    start, weights, outs = refs[:begins], refs[begins : begins + len(depths)], refs[begins + len(depths) :]
    rows = acts[0].shape[0]
    width = 256 if outs[0].shape[1] % 256 == 0 else 128
    for column in range(0, outs[0].shape[1], width):
        columns = slice(column, column + width)
        for j, a in enumerate(acts):
            total = start[0][j * rows : (j + 1) * rows, columns] if start else None
            at = skip
            for n, (w, depth) in enumerate(zip(weights, depths)):
                first = column + (0 if n or start else shift)
                term = dot(a[:rows, at : at + depth], w[:depth, first : first + width])
                total = term if total is None else total + term
                at += depth
            if len(outs) == 1:
                outs[0][j * rows : (j + 1) * rows, columns] = total
            else:
                place = slice((j // 2) * rows, (j // 2 + 1) * rows)
                outs[j % 2][place, columns] = total.astype(outs[j % 2].dtype)


def project(acts, skip, shift, weights, depths, columns, start=(), last=True):
    rows = acts[0].shape[0]
    if last:
        out = [(2 * rows, jnp.float32), (2 * rows, jnp.bfloat16)]
    else:
        out = [(GROUP * rows, jnp.float32)]
    return pl.pallas_call(
        functools.partial(project_kernel, skip, shift, depths, len(start)),
        out_shape=[jax.ShapeDtypeStruct((n, columns), t) for n, t in out],
        in_specs=[whole()] * (len(acts) + len(start) + len(weights)),
        out_specs=[whole()] * len(out),
        compiler_params=params(),
        cost_estimate=pl.CostEstimate(
            flops=2 * GROUP * rows * sum(depths) * columns,
            bytes_accessed=2 * sum(depths) * (GROUP * rows + columns) + 6 * GROUP * rows * columns,
            transcendentals=0,
        ),
        name="project",
    )(*acts, *start, *weights)


def by_request(*shape):
    return pl.BlockSpec((1, *shape), lambda r: (r,) + (0,) * len(shape))


def against(a, b, dims):
    return lax.dot_general(a, b, (dims, ((), ())), preferred_element_type=jnp.float32)

def stacked_queries(q_ref, group):
    heads = []
    for i in range(HEAD_GROUP):
        at = (group * HEAD_GROUP + i) * HEAD_SIZE
        heads.append(q_ref[0, :, at : at + HEAD_SIZE].astype(jnp.float32))
    return jnp.concatenate(heads, axis=0).astype(jnp.bfloat16)


def cached_kernel(per_dev, maxp, place_ref, home_ref, ids_ref, rows_ref, count_ref, q_ref, *refs):
    sources, (query_pos_ref, out_ref, stat_ref, stacked_ref, pages, context, bias, sems) = refs[:-8], refs[-8:]
    r = pl.program_id(0)
    plen = context.shape[1] // maxp
    per_pass = q_ref.shape[1] // maxp

    @pl.when(r == 0)
    def _():
        copies = []
        at = 0
        for n, source in enumerate(sources):
            rows = source.shape[0]
            copies.append(pltpu.make_async_copy(source, pages.at[pl.ds(at, rows)], sems.at[n]))
            at += rows
        for copy in copies:
            copy.start()
        for copy in copies:
            copy.wait()

    for m in range(maxp):
        slot = home_ref[ids_ref[r * maxp + m]]
        block = place_ref[slot // per_dev] * (2 * per_dev) + slot % per_dev
        for c in range(2):
            at = pl.multiple_of((block + c * per_dev) * plen, plen)
            context[c, m * plen : (m + 1) * plen, :] = pages[pl.ds(at, plen), :]
    row = lax.broadcasted_iota(jnp.int32, (plen, bias.shape[1]), 0)
    for m in range(maxp):
        hidden = m >= count_ref[r]
        for i in range(per_pass):
            hidden = hidden | (row == rows_ref[(r * maxp + m) * per_pass + i])
        key_pos = jnp.where(hidden, NEVER, row + m * plen)
        bias[m * plen : (m + 1) * plen, :] = jnp.where(key_pos <= query_pos_ref[0], 0.0, HIDDEN)
    heads = [slice(g * HEAD_SIZE, (g + 1) * HEAD_SIZE) for g in range(KEY_VALUE_HEADS)]
    scores = []
    for g, head in enumerate(heads):
        q = stacked_queries(q_ref, g)
        stacked_ref[0, g] = q
        scores.append(against(context[0, :, head], q, ((1,), (1,))))
    weights = []
    for g, s in enumerate(scores):
        s = s * EXP2_SCALE + bias[...]
        top = jnp.max(s, axis=0, keepdims=True)
        e = jnp.exp2(s - top)
        stat_ref[0, g, 0:1] = top
        stat_ref[0, g, 1:2] = jnp.sum(e, axis=0, keepdims=True)
        weights.append(e.astype(jnp.bfloat16))
    for g, head in enumerate(heads):
        out_ref[0, g] = against(context[1, :, head], weights[g], ((0,), (0,)))


def cached_attention(per_dev, maxp, plen, place, home, ids, sources, rows, count, queries, query_pos):
    owned, selected, width = queries.shape
    stacked = HEAD_GROUP * selected
    context = maxp * plen
    features = sources[0].shape[1]
    heads = KEY_VALUE_HEADS
    return pl.pallas_call(
        functools.partial(cached_kernel, per_dev, maxp),
        out_shape=[
            jax.ShapeDtypeStruct((owned, heads, HEAD_SIZE, stacked), jnp.float32),
            jax.ShapeDtypeStruct((owned, heads, 2, stacked), jnp.float32),
            jax.ShapeDtypeStruct((owned, heads, stacked, HEAD_SIZE), jnp.bfloat16),
        ],
        grid=(owned,),
        in_specs=[
            *[smem()] * 5,
            by_request(selected, width),
            *[pl.BlockSpec(memory_space=pl.ANY)] * len(sources),
            by_request(1, stacked),
        ],
        out_specs=[
            by_request(heads, HEAD_SIZE, stacked),
            by_request(heads, 2, stacked),
            by_request(heads, stacked, HEAD_SIZE),
        ],
        scratch_shapes=[
            pltpu.VMEM((sum(x.shape[0] for x in sources), features), jnp.bfloat16),
            pltpu.VMEM((2, context, features), jnp.bfloat16),
            pltpu.VMEM((context, stacked), jnp.float32),
            pltpu.SemaphoreType.DMA((len(sources),)),
        ],
        compiler_params=params(),
        cost_estimate=pl.CostEstimate(
            flops=4 * queries.size * context,
            bytes_accessed=4 * queries.size + 8 * sources[0].size,
            transcendentals=owned * heads * stacked * context,
        ),
        name="cached_attention",
    )(place, home, ids, rows, count, queries, *sources, query_pos)


def added(own_ref, *others):
    total = own_ref[0]
    for other in others:
        total = total + other[0].astype(jnp.float32)
    return total.astype(jnp.bfloat16)


def fresh_kernel(maxp, count_ref, q_ref, *refs):
    terms, (query_pos_ref, part_ref, stat_ref, out_ref) = refs[:-4], refs[-4:]
    r = pl.program_id(0)
    half = len(terms) // 2
    fresh = jnp.concatenate([added(*terms[:half]), added(*terms[half:])], axis=1)
    fresh_keys, fresh_values = fresh[:, : fresh.shape[1] // 2], fresh[:, fresh.shape[1] // 2 :]
    rows = fresh_keys.shape[0]
    per_pass = rows // maxp
    slot = lax.broadcasted_iota(jnp.int32, (rows, HEAD_SIZE), 0) // per_pass
    live = slot < count_ref[r]
    across = jnp.broadcast_to(query_pos_ref[0, :, :HEAD_SIZE], (HEAD_SIZE, HEAD_SIZE))
    key_pos = jnp.where(live, across.T[:rows], NEVER)[:, :1]
    bias = jnp.where(key_pos <= query_pos_ref[0], 0.0, HIDDEN)
    heads = [slice(g * HEAD_SIZE, (g + 1) * HEAD_SIZE) for g in range(KEY_VALUE_HEADS)]
    scores = [against(fresh_keys[:, head], q_ref[0, g], ((1,), (1,))) for g, head in enumerate(heads)]
    weights, factors = [], []
    for g, s in enumerate(scores):
        s = s * EXP2_SCALE + bias
        top1 = stat_ref[0, g, 0:1]
        top = jnp.maximum(top1, jnp.max(s, axis=0, keepdims=True))
        e = jnp.exp2(s - top)
        keep = jnp.exp2(top1 - top)
        total = stat_ref[0, g, 1:2] * keep + jnp.sum(e, axis=0, keepdims=True)
        weights.append(e.astype(jnp.bfloat16))
        factors.append((keep, 1.0 / total))
    terms = [against(fresh_values[:, head], weights[g], ((0,), (0,))) for g, head in enumerate(heads)]
    for g, (keep, inv) in enumerate(factors):
        result = ((part_ref[0, g] * keep + terms[g]) * inv).T
        for i in range(HEAD_GROUP):
            at = (g * HEAD_GROUP + i) * HEAD_SIZE
            one = result[i * rows : (i + 1) * rows]
            out_ref[0, :, at : at + HEAD_SIZE] = jnp.where(live, one, 0.0).astype(jnp.bfloat16)


def fresh_attention(maxp, count, queries, terms, query_pos, part, stat):
    owned, heads, stacked, _ = queries.shape
    rows = terms[0].shape[1]
    width = QUERY_HEADS * HEAD_SIZE
    return pl.pallas_call(
        functools.partial(fresh_kernel, maxp),
        out_shape=jax.ShapeDtypeStruct((owned, rows, width), jnp.bfloat16),
        grid=(owned,),
        in_specs=[
            smem(),
            by_request(heads, stacked, HEAD_SIZE),
            *[by_request(*t.shape[1:]) for t in terms],
            by_request(1, stacked),
            by_request(heads, HEAD_SIZE, stacked),
            by_request(heads, 2, stacked),
        ],
        out_specs=by_request(rows, width),
        compiler_params=params(),
        cost_estimate=pl.CostEstimate(
            flops=4 * queries.size * rows,
            bytes_accessed=8 * queries.size,
            transcendentals=owned * heads * stacked * rows,
        ),
        name="fresh_attention",
    )(count, queries, *terms, query_pos, part, stat)


def query_positions(rows, plen):
    owned, maxp, per_pass = rows.shape
    slot = jnp.arange(maxp * per_pass, dtype=jnp.int32) // per_pass
    at = slot * plen + rows.reshape(owned, maxp * per_pass)
    return jnp.tile(at, (1, HEAD_GROUP))[:, None, :]


def together(*arrays):
    return lax.optimization_barrier(arrays)


def after(x, *earlier):
    return lax.optimization_barrier((x, *earlier))[0]


def ring_plan(rows_in, norm_gain, kv_weight, store_pages, small):
    shards = lax.axis_size("store")
    me = lax.axis_index("store")
    side = lax.axis_index("parts")
    ring = shards // GROUP
    z, member = me // GROUP, me % GROUP
    owned, selected, width = rows_in.shape
    depth, features = kv_weight.shape
    local, plen, _, kvw = store_pages.shape
    half = depth // 2
    split = features // 2
    count = owned * selected

    pages = store_pages.reshape(local * plen, 2, kvw)
    mine = [
        lax.dynamic_slice(kv_weight, (side * half, first), (half, columns))
        for first, columns in ((0, split), (split, features - split))
    ]
    own = jnp.concatenate([pages[:, 0], pages[:, 1]], axis=0)
    a0 = jnp.concatenate([mine[0], own], axis=0)
    a1 = send(a0, 1)
    b1 = send(mine[1], 1)

    steps = jnp.arange(2 * ring, dtype=jnp.int32) // 2
    blocks = (z - steps) % ring
    halves = jnp.arange(2 * ring, dtype=jnp.int32) % 2
    halves = jnp.where(steps == 0, halves, halves ^ side)
    targets = member ^ jnp.arange(GROUP, dtype=jnp.int32)
    offs = (blocks[None] * GROUP + targets[:, None]) * depth + halves[None] * half
    offs = (offs // 128).reshape(-1)

    device = jnp.arange(shards, dtype=jnp.int32)
    rank = (z - device // GROUP) % ring
    rel = (device % GROUP) ^ member
    place = ((rel % 2) * 2 + rel // 2) * ring + rank
    acts = norm_rows(rows_in.reshape(count, width), norm_gain, after(offs, a0), half)
    y_acts = flip(after(acts[1], b1), 2)
    near_act = flip(acts[2], 1)
    a1, near_act, place, *small = together(a1, near_act, place, *small)
    a2 = send(after(a1, b1), 1)
    xa1 = swap(after(a1[:half], near_act))
    b2 = send(after(b1, near_act), 1)
    xb1 = swap(b1)
    a3 = send(after(a2, xa1), 1)
    xa2 = swap(after(a2[:half], xa1))
    b3 = send(after(b2, xb1), 1)
    xb2 = swap(after(b2, xb1))
    y_far = flip(y_acts[count:], 1)
    xa3 = swap(after(a3[:half], xa2))
    xb3 = swap(after(b3, xb2))
    column = jnp.concatenate([own, a1[half:], a2[half:], a3[half:]], axis=0)
    y_column = flip(after(column, y_acts), 2)
    far = flip(after(column, b3), 1)
    y_column_far = flip(y_column, 1)
    acts = [acts[0], near_act, y_acts, y_far]

    depths = (depth,) + (half,) * (2 * ring - 2)
    terms = []
    begun = project(acts, 0, 0, [kv_weight, a1, xa1, a2, xa2, a3], depths[:-1], split, (), False)
    keep, out = project(acts, width // GROUP - half, 0, [xa3], depths[-1:], split, begun)
    back = flip(out, 1)
    y_out = (keep[count:] + back[count:].astype(jnp.float32)).astype(jnp.bfloat16)
    terms += [keep, back, flip(y_out, 2)]
    keep, out = project(acts, 0, split, [kv_weight, b1, xb1, b2, xb2, b3, xb3], depths, features - split)
    back = flip(out, 1)
    y_out = (keep[count:] + back[count:].astype(jnp.float32)).astype(jnp.bfloat16)
    terms += [keep, back, flip(y_out, 2)]
    return small, (place, [column, y_column, far, y_column_far]), terms


def gathered_projection(rows_in, norm_gain, kv_weight):
    owned, selected, width = rows_in.shape
    wide = rows_in.reshape(owned * selected, width).astype(jnp.float32)
    inv = lax.rsqrt(jnp.mean(wide * wide, axis=-1, keepdims=True) + 1e-05)
    normed = (wide * inv * norm_gain.astype(jnp.float32)).astype(jnp.bfloat16)
    fresh = dot(normed, lax.all_gather(kv_weight, "store", axis=0, tiled=True))
    none = jnp.zeros((fresh.shape[0], fresh.shape[1] // 2), jnp.bfloat16)
    keys, values = jnp.split(fresh, 2, axis=1)
    return [keys, none, none, values, none, none]


def sent_pages(store_pages, passage_home, passage_ids):
    shards = lax.axis_size("store")
    me = lax.axis_index("store")
    local, plen, _, kvw = store_pages.shape
    owned = passage_ids.shape[0] // shards
    positions = owned * passage_ids.shape[1]
    cap = (positions + shards - 1) // shards
    slots = passage_home[passage_ids]
    home_shard = (slots // local).reshape(shards, positions)
    local_slot = (slots % local).reshape(shards, positions)
    earlier = jnp.tril(jnp.ones((positions, positions), jnp.bool_), -1)
    same = home_shard[:, :, None] == home_shard[:, None, :]
    rank = jnp.sum(same & earlier[None], axis=2)
    ladder = jnp.arange(cap, dtype=jnp.int32)
    hit = (home_shard[:, :, None] == me) & (rank[:, :, None] == ladder[None, None, :])
    pick = jnp.sum(jnp.where(hit, local_slot[:, :, None], 0), axis=1)
    outgoing = store_pages[pick.reshape(shards * cap)]
    my_shard = lax.dynamic_slice_in_dim(home_shard, me, 1, 0)[0]
    my_rank = lax.dynamic_slice_in_dim(rank, me, 1, 0)[0]
    arrived = lax.all_to_all(outgoing, "store", split_axis=0, concat_axis=0, tiled=True)
    arrived = arrived.transpose(0, 2, 1, 3).reshape(shards * cap * 2 * plen, kvw)
    place = jnp.arange(shards * cap, dtype=jnp.int32)
    home = (my_shard * cap + my_rank).astype(jnp.int32)
    ids = jnp.arange(positions, dtype=jnp.int32)
    return place, home, ids, [arrived]


def per_device(
    rows_in,
    norm_gain,
    kv_weight,
    queries,
    store_pages,
    passage_home,
    passage_ids,
    passage_count,
    recompute_rows,
):
    shards = lax.axis_size("store")
    me = lax.axis_index("store")
    owned, selected, _ = rows_in.shape
    local, plen = store_pages.shape[:2]
    ringed = shards == 4 * GROUP and lax.axis_size("parts") == 2 and kv_weight.shape[0] % 512 == 0
    rows = lax.dynamic_slice_in_dim(recompute_rows, me * owned, owned, 0)
    query_pos = query_positions(rows, plen)
    flat_rows = rows.reshape(-1)
    maxp = passage_ids.shape[1]
    if ringed:
        ids = lax.dynamic_slice_in_dim(passage_ids, me * owned, owned, 0).reshape(-1)
        small, (place, sources), terms = ring_plan(
            rows_in, norm_gain, kv_weight, store_pages, [ids, flat_rows, query_pos]
        )
        ids, flat_rows, query_pos = small
        pages = (place, passage_home, ids, sources)
        per_dev = local
    else:
        terms = gathered_projection(rows_in, norm_gain, kv_weight)
        pages = sent_pages(store_pages, passage_home, passage_ids)
        per_dev = 1
    part, stat, stacked = cached_attention(
        per_dev, maxp, plen, *pages, flat_rows, passage_count, queries, query_pos
    )
    terms = [t.reshape(-1, selected, t.shape[1]) for t in terms]
    return fresh_attention(maxp, passage_count, stacked, terms, query_pos, part, stat)


def solution(mesh):
    in_specs = (
        P(("parts", "store"), None, None),
        P(),
        P("store", None),
        P(("parts", "store"), None, None),
        P(("parts", "store"), None, None, None),
        P("parts"),
        P("parts", None),
        P(("parts", "store")),
        P("parts", None, None),
    )
    out_specs = P(("parts", "store"), None, None)
    return jax.shard_map(
        per_device, mesh=mesh, in_specs=in_specs, out_specs=out_specs, check_vma=False
    )
```

```python
import functools
import math

import jax
import jax.numpy as jnp
from jax import lax
from jax.experimental import pallas as pl
from jax.experimental.pallas import tpu as pltpu
from jax.sharding import PartitionSpec as P

QUERY_HEADS = 32
KEY_VALUE_HEADS = 4
HEAD_SIZE = 128
HEAD_GROUP = QUERY_HEADS // KEY_VALUE_HEADS
GROUP = 4
HIDDEN = -1e30
NEVER = 1 << 30
EXP2_SCALE = math.log2(math.e) / math.sqrt(HEAD_SIZE)
VMEM_LIMIT = 16 * 2**20


def params(**more):
    return pltpu.CompilerParams(vmem_limit_bytes=VMEM_LIMIT, **more)


def whole():
    return pl.BlockSpec(memory_space=pltpu.VMEM)


def smem():
    return pl.BlockSpec(memory_space=pltpu.SMEM)


def send(x, steps):
    shards = lax.axis_size("store")
    pairs = [(i, (i + steps * GROUP) % shards) for i in range(shards)]
    return lax.ppermute(x, "store", pairs)


def flip(x, bits):
    pairs = [(i, i ^ bits) for i in range(lax.axis_size("store"))]
    return lax.ppermute(x, "store", pairs)


def swap(x):
    return lax.ppermute(x, "parts", [(0, 1), (1, 0)])


def norm_kernel(chunk, chunks, offs_ref, rows_ref, gain_ref, own_ref, y_ref, core_ref, held):
    wide = rows_ref[...].astype(jnp.float32)
    inv = lax.rsqrt(jnp.mean(wide * wide, axis=-1, keepdims=True) + 1e-05)
    held[...] = (wide * inv * gain_ref[...].astype(jnp.float32)).astype(jnp.bfloat16)
    for j in range(GROUP):
        for k in range(chunks):
            at = pl.multiple_of(offs_ref[j * chunks + k] * 128, 128)
            piece = held[:, pl.ds(at, chunk)]
            if j < 2:
                out = (own_ref, core_ref)[j]
                out[:, k * chunk : (k + 1) * chunk] = piece
            else:
                y_ref[j - 2, :, k * chunk : (k + 1) * chunk] = piece


def norm_rows(rows, gain, offs, chunk):
    count, width = rows.shape
    chunks = width // GROUP // chunk
    block = 32
    depth = width // GROUP
    one = jax.ShapeDtypeStruct((count, depth), jnp.bfloat16)
    two = jax.ShapeDtypeStruct((2, count, depth), jnp.bfloat16)
    one_spec = pl.BlockSpec((block, depth), lambda i: (i, 0))
    own, y, core = pl.pallas_call(
        functools.partial(norm_kernel, chunk, chunks),
        out_shape=[one, two, one],
        grid=(count // block,),
        in_specs=[
            smem(),
            pl.BlockSpec((block, width), lambda i: (i, 0)),
            pl.BlockSpec((1, width), lambda i: (0, 0)),
        ],
        out_specs=[one_spec, pl.BlockSpec((2, block, depth), lambda i: (0, i, 0)), one_spec],
        scratch_shapes=[pltpu.VMEM((block, width), jnp.bfloat16)],
        compiler_params=params(),
        cost_estimate=pl.CostEstimate(
            flops=6 * count * width, bytes_accessed=4 * count * width, transcendentals=0
        ),
        name="norm",
    )(offs, rows, gain.reshape(1, width))
    return own, y.reshape(2 * count, depth), core


def dot(a, b):
    return jnp.dot(a, b, preferred_element_type=jnp.float32)


def project_kernel(skip, shift, depths, begins, *refs):
    acts, refs = refs[:GROUP], refs[GROUP:]
    start, weights, outs = refs[:begins], refs[begins : begins + len(depths)], refs[begins + len(depths) :]
    rows = acts[0].shape[0]
    width = 256 if outs[0].shape[1] % 256 == 0 else 128
    for column in range(0, outs[0].shape[1], width):
        columns = slice(column, column + width)
        for j, a in enumerate(acts):
            total = start[0][j * rows : (j + 1) * rows, columns] if start else None
            at = skip
            for n, (w, depth) in enumerate(zip(weights, depths)):
                first = column + (0 if n or start else shift)
                term = dot(a[:rows, at : at + depth], w[:depth, first : first + width])
                total = term if total is None else total + term
                at += depth
            if len(outs) == 1:
                outs[0][j * rows : (j + 1) * rows, columns] = total
            else:
                place = slice((j // 2) * rows, (j // 2 + 1) * rows)
                outs[j % 2][place, columns] = total.astype(outs[j % 2].dtype)


def project(acts, skip, shift, weights, depths, columns, start=(), last=True):
    rows = acts[0].shape[0]
    if last:
        out = [(2 * rows, jnp.float32), (2 * rows, jnp.bfloat16)]
    else:
        out = [(GROUP * rows, jnp.float32)]
    return pl.pallas_call(
        functools.partial(project_kernel, skip, shift, depths, len(start)),
        out_shape=[jax.ShapeDtypeStruct((n, columns), t) for n, t in out],
        in_specs=[whole()] * (len(acts) + len(start) + len(weights)),
        out_specs=[whole()] * len(out),
        compiler_params=params(),
        cost_estimate=pl.CostEstimate(
            flops=2 * GROUP * rows * sum(depths) * columns,
            bytes_accessed=2 * sum(depths) * (GROUP * rows + columns) + 6 * GROUP * rows * columns,
            transcendentals=0,
        ),
        name="project",
    )(*acts, *start, *weights)


def by_request(*shape):
    return pl.BlockSpec((1, *shape), lambda r: (r,) + (0,) * len(shape))


def against(a, b, dims):
    return lax.dot_general(a, b, (dims, ((), ())), preferred_element_type=jnp.float32)

def stacked_queries(q_ref, group):
    heads = []
    for i in range(HEAD_GROUP):
        at = (group * HEAD_GROUP + i) * HEAD_SIZE
        heads.append(q_ref[0, :, at : at + HEAD_SIZE].astype(jnp.float32))
    return jnp.concatenate(heads, axis=0).astype(jnp.bfloat16)


def cached_kernel(per_dev, maxp, place_ref, home_ref, ids_ref, rows_ref, count_ref, q_ref, *refs):
    sources, (query_pos_ref, out_ref, stat_ref, stacked_ref, pages, context, bias, sems) = refs[:-8], refs[-8:]
    r = pl.program_id(0)
    plen = context.shape[1] // maxp
    per_pass = q_ref.shape[1] // maxp

    @pl.when(r == 0)
    def _():
        copies = []
        at = 0
        for n, source in enumerate(sources):
            rows = source.shape[0]
            copies.append(pltpu.make_async_copy(source, pages.at[pl.ds(at, rows)], sems.at[n]))
            at += rows
        for copy in copies:
            copy.start()
        for copy in copies:
            copy.wait()

    for m in range(maxp):
        slot = home_ref[ids_ref[r * maxp + m]]
        block = place_ref[slot // per_dev] * (2 * per_dev) + slot % per_dev
        for c in range(2):
            at = pl.multiple_of((block + c * per_dev) * plen, plen)
            context[c, m * plen : (m + 1) * plen, :] = pages[pl.ds(at, plen), :]
    row = lax.broadcasted_iota(jnp.int32, (plen, bias.shape[1]), 0)
    for m in range(maxp):
        hidden = m >= count_ref[r]
        for i in range(per_pass):
            hidden = hidden | (row == rows_ref[(r * maxp + m) * per_pass + i])
        key_pos = jnp.where(hidden, NEVER, row + m * plen)
        bias[m * plen : (m + 1) * plen, :] = jnp.where(key_pos <= query_pos_ref[0], 0.0, HIDDEN)
    heads = [slice(g * HEAD_SIZE, (g + 1) * HEAD_SIZE) for g in range(KEY_VALUE_HEADS)]
    scores = []
    for g, head in enumerate(heads):
        q = stacked_queries(q_ref, g)
        stacked_ref[0, g] = q
        scores.append(against(context[0, :, head], q, ((1,), (1,))))
    weights = []
    for g, s in enumerate(scores):
        s = s * EXP2_SCALE + bias[...]
        top = jnp.max(s, axis=0, keepdims=True)
        e = jnp.exp2(s - top)
        stat_ref[0, g, 0:1] = top
        stat_ref[0, g, 1:2] = jnp.sum(e, axis=0, keepdims=True)
        weights.append(e.astype(jnp.bfloat16))
    for g, head in enumerate(heads):
        out_ref[0, g] = against(context[1, :, head], weights[g], ((0,), (0,)))


def cached_attention(per_dev, maxp, plen, place, home, ids, sources, rows, count, queries, query_pos):
    owned, selected, width = queries.shape
    stacked = HEAD_GROUP * selected
    context = maxp * plen
    features = sources[0].shape[1]
    heads = KEY_VALUE_HEADS
    return pl.pallas_call(
        functools.partial(cached_kernel, per_dev, maxp),
        out_shape=[
            jax.ShapeDtypeStruct((owned, heads, HEAD_SIZE, stacked), jnp.float32),
            jax.ShapeDtypeStruct((owned, heads, 2, stacked), jnp.float32),
            jax.ShapeDtypeStruct((owned, heads, stacked, HEAD_SIZE), jnp.bfloat16),
        ],
        grid=(owned,),
        in_specs=[
            *[smem()] * 5,
            by_request(selected, width),
            *[pl.BlockSpec(memory_space=pl.ANY)] * len(sources),
            by_request(1, stacked),
        ],
        out_specs=[
            by_request(heads, HEAD_SIZE, stacked),
            by_request(heads, 2, stacked),
            by_request(heads, stacked, HEAD_SIZE),
        ],
        scratch_shapes=[
            pltpu.VMEM((sum(x.shape[0] for x in sources), features), jnp.bfloat16),
            pltpu.VMEM((2, context, features), jnp.bfloat16),
            pltpu.VMEM((context, stacked), jnp.float32),
            pltpu.SemaphoreType.DMA((len(sources),)),
        ],
        compiler_params=params(),
        cost_estimate=pl.CostEstimate(
            flops=4 * queries.size * context,
            bytes_accessed=4 * queries.size + 8 * sources[0].size,
            transcendentals=owned * heads * stacked * context,
        ),
        name="cached_attention",
    )(place, home, ids, rows, count, queries, *sources, query_pos)


def added(own_ref, *others):
    total = own_ref[0]
    for other in others:
        total = total + other[0].astype(jnp.float32)
    return total.astype(jnp.bfloat16)


def scores_kernel(maxp, count_ref, q_ref, *refs):
    terms, (query_pos_ref, stat_ref, part_ref, weight_ref, base_ref) = refs[:-5], refs[-5:]
    count = count_ref[pl.program_id(0)]
    fresh_keys = added(*terms)
    rows = fresh_keys.shape[0]
    per_pass = rows // maxp
    slot = lax.broadcasted_iota(jnp.int32, (rows, HEAD_SIZE), 0) // per_pass
    across = jnp.broadcast_to(query_pos_ref[0, :, :HEAD_SIZE], (HEAD_SIZE, HEAD_SIZE))
    key_pos = jnp.where(slot < count, across.T[:rows], NEVER)[:, :1]
    bias = jnp.where(key_pos <= query_pos_ref[0], 0.0, HIDDEN)
    query = lax.broadcasted_iota(jnp.int32, query_pos_ref.shape[1:], 1)
    live = query % rows // per_pass < count
    heads = [slice(g * HEAD_SIZE, (g + 1) * HEAD_SIZE) for g in range(KEY_VALUE_HEADS)]
    scores = [against(fresh_keys[:, head], q_ref[0, g], ((1,), (1,))) for g, head in enumerate(heads)]
    for g, s in enumerate(scores):
        s = s * EXP2_SCALE + bias
        top1 = stat_ref[0, g, 0:1]
        top = jnp.maximum(top1, jnp.max(s, axis=0, keepdims=True))
        e = jnp.exp2(s - top)
        keep = jnp.exp2(top1 - top)
        inv = 1.0 / (stat_ref[0, g, 1:2] * keep + jnp.sum(e, axis=0, keepdims=True))
        inv = jnp.where(live, inv, 0.0)
        weight_ref[0, g] = (e * inv).astype(jnp.bfloat16)
        base_ref[0, g] = (part_ref[0, g] * (keep * inv)).T


def fresh_scores(maxp, count, queries, terms, query_pos, part, stat):
    owned, heads, stacked, _ = queries.shape
    rows = terms[0].shape[1]
    return pl.pallas_call(
        functools.partial(scores_kernel, maxp),
        out_shape=[
            jax.ShapeDtypeStruct((owned, heads, rows, stacked), jnp.bfloat16),
            jax.ShapeDtypeStruct((owned, heads, stacked, HEAD_SIZE), jnp.float32),
        ],
        grid=(owned,),
        in_specs=[
            smem(),
            by_request(heads, stacked, HEAD_SIZE),
            *[by_request(*t.shape[1:]) for t in terms],
            by_request(1, stacked),
            by_request(heads, 2, stacked),
            by_request(heads, HEAD_SIZE, stacked),
        ],
        out_specs=[by_request(heads, rows, stacked), by_request(heads, stacked, HEAD_SIZE)],
        compiler_params=params(),
        cost_estimate=pl.CostEstimate(
            flops=2 * queries.size * rows,
            bytes_accessed=8 * part.size,
            transcendentals=owned * heads * stacked * rows,
        ),
        name="fresh_scores",
    )(count, queries, *terms, query_pos, stat, part)


def values_kernel(*refs):
    terms, (weight_ref, base_ref, out_ref) = refs[:-3], refs[-3:]
    fresh_values = added(*terms)
    rows = fresh_values.shape[0]
    heads = [slice(g * HEAD_SIZE, (g + 1) * HEAD_SIZE) for g in range(KEY_VALUE_HEADS)]
    sums = [against(weight_ref[0, g], fresh_values[:, head], ((0,), (0,))) for g, head in enumerate(heads)]
    for g, fresh in enumerate(sums):
        result = base_ref[0, g] + fresh
        for i in range(HEAD_GROUP):
            at = (g * HEAD_GROUP + i) * HEAD_SIZE
            out_ref[0, :, at : at + HEAD_SIZE] = result[i * rows : (i + 1) * rows].astype(jnp.bfloat16)


def fresh_attention(weights, terms, base):
    owned, heads, rows, stacked = weights.shape
    width = QUERY_HEADS * HEAD_SIZE
    return pl.pallas_call(
        values_kernel,
        out_shape=jax.ShapeDtypeStruct((owned, rows, width), jnp.bfloat16),
        grid=(owned,),
        in_specs=[
            *[by_request(*t.shape[1:]) for t in terms],
            by_request(heads, rows, stacked),
            by_request(heads, stacked, HEAD_SIZE),
        ],
        out_specs=by_request(rows, width),
        compiler_params=params(),
        cost_estimate=pl.CostEstimate(
            flops=2 * owned * rows * width * rows,
            bytes_accessed=4 * base.size + 2 * owned * rows * width,
            transcendentals=0,
        ),
        name="fresh_attention",
    )(*terms, weights, base)


def query_positions(rows, plen):
    owned, maxp, per_pass = rows.shape
    slot = jnp.arange(maxp * per_pass, dtype=jnp.int32) // per_pass
    at = slot * plen + rows.reshape(owned, maxp * per_pass)
    return jnp.tile(at, (1, HEAD_GROUP))[:, None, :]


def together(*arrays):
    return lax.optimization_barrier(arrays)


def after(x, *earlier):
    return lax.optimization_barrier((x, *earlier))[0]


def ring_plan(rows_in, norm_gain, kv_weight, store_pages, small):
    shards = lax.axis_size("store")
    me = lax.axis_index("store")
    side = lax.axis_index("parts")
    ring = shards // GROUP
    z, member = me // GROUP, me % GROUP
    owned, selected, width = rows_in.shape
    depth, features = kv_weight.shape
    local, plen, _, kvw = store_pages.shape
    half = depth // 2
    split = features // 2
    count = owned * selected

    pages = store_pages.reshape(local * plen, 2, kvw)
    mine = [
        lax.dynamic_slice(kv_weight, (side * half, first), (half, columns))
        for first, columns in ((split, features - split), (0, split))
    ]
    own = jnp.concatenate([pages[:, 0], pages[:, 1]], axis=0)
    a0 = mine[0]
    b0 = jnp.concatenate([mine[1], own], axis=0)
    a1 = send(a0, 1)
    b1 = send(b0, 1)

    steps = jnp.array([0, 0, 1, 1, 3, 3, 2, 2], jnp.int32)
    blocks = (z - steps) % ring
    halves = jnp.arange(2 * ring, dtype=jnp.int32) % 2
    halves = jnp.where(steps == 0, halves, halves ^ side)
    targets = member ^ jnp.arange(GROUP, dtype=jnp.int32)
    offs = (blocks[None] * GROUP + targets[:, None]) * depth + halves[None] * half
    offs = (offs // 128).reshape(-1)

    device = jnp.arange(shards, dtype=jnp.int32)
    rank = (z - device // GROUP) % ring
    rel = (device % GROUP) ^ member
    place = ((rel % 2) * 2 + rel // 2) * ring + rank
    acts = norm_rows(rows_in.reshape(count, width), norm_gain, after(offs, b0), half)
    y_acts = flip(after(acts[1], a1), 2)
    near_act = flip(acts[2], 1)
    a1, near_act, place, *small = together(a1, near_act, place, *small)
    b3 = send(after(b0, b1, a1), -1)
    xb1 = swap(after(b1[:half], near_act))
    a3 = send(after(a0, near_act, a1), -1)
    xa1 = swap(a1)
    b2 = send(after(b1, b3), 1)
    xb3 = swap(after(b3[:half], xb1))
    a2 = send(after(a1, xa1), 1)
    xa3 = swap(after(a3, xa1))
    y_far = flip(y_acts[count:], 1)
    xb2 = swap(after(b2[:half], xb3))
    xa2 = swap(after(a2, xa3))
    column = jnp.concatenate([own, b1[half:], b2[half:], b3[half:]], axis=0)
    y_column = flip(after(column, y_acts), 2)
    far = flip(column, 1)
    y_column_far = flip(after(y_column, xb2), 1)
    acts = [acts[0], near_act, y_acts, y_far]

    depths = (depth,) + (half,) * (2 * ring - 2)
    terms = []
    begun = project(acts, 0, 0, [kv_weight, b1, xb1, b3, xb3, b2], depths[:-1], split, (), False)
    keep, out = project(acts, width // GROUP - half, 0, [xb2], depths[-1:], split, begun)
    back = flip(out, 1)
    y_out = (keep[count:] + back[count:].astype(jnp.float32)).astype(jnp.bfloat16)
    terms += [keep, back, flip(y_out, 2)]
    begun = project(acts, 0, split, [kv_weight, a1, xa1, a3, xa3, a2], depths[:-1], features - split, (), False)
    keep, out = project(acts, width // GROUP - half, 0, [xa2], depths[-1:], features - split, begun)
    back = flip(out, 1)
    y_out = (keep[count:] + back[count:].astype(jnp.float32)).astype(jnp.bfloat16)
    terms += [keep, back, flip(y_out, 2)]
    return small, (place, [column, y_column, far, y_column_far]), terms


def gathered_projection(rows_in, norm_gain, kv_weight):
    owned, selected, width = rows_in.shape
    wide = rows_in.reshape(owned * selected, width).astype(jnp.float32)
    inv = lax.rsqrt(jnp.mean(wide * wide, axis=-1, keepdims=True) + 1e-05)
    normed = (wide * inv * norm_gain.astype(jnp.float32)).astype(jnp.bfloat16)
    fresh = dot(normed, lax.all_gather(kv_weight, "store", axis=0, tiled=True))
    none = jnp.zeros((fresh.shape[0], fresh.shape[1] // 2), jnp.bfloat16)
    keys, values = jnp.split(fresh, 2, axis=1)
    return [keys, none, none, values, none, none]


def sent_pages(store_pages, passage_home, passage_ids):
    shards = lax.axis_size("store")
    me = lax.axis_index("store")
    local, plen, _, kvw = store_pages.shape
    owned = passage_ids.shape[0] // shards
    positions = owned * passage_ids.shape[1]
    cap = (positions + shards - 1) // shards
    slots = passage_home[passage_ids]
    home_shard = (slots // local).reshape(shards, positions)
    local_slot = (slots % local).reshape(shards, positions)
    earlier = jnp.tril(jnp.ones((positions, positions), jnp.bool_), -1)
    same = home_shard[:, :, None] == home_shard[:, None, :]
    rank = jnp.sum(same & earlier[None], axis=2)
    ladder = jnp.arange(cap, dtype=jnp.int32)
    hit = (home_shard[:, :, None] == me) & (rank[:, :, None] == ladder[None, None, :])
    pick = jnp.sum(jnp.where(hit, local_slot[:, :, None], 0), axis=1)
    outgoing = store_pages[pick.reshape(shards * cap)]
    my_shard = lax.dynamic_slice_in_dim(home_shard, me, 1, 0)[0]
    my_rank = lax.dynamic_slice_in_dim(rank, me, 1, 0)[0]
    arrived = lax.all_to_all(outgoing, "store", split_axis=0, concat_axis=0, tiled=True)
    arrived = arrived.transpose(0, 2, 1, 3).reshape(shards * cap * 2 * plen, kvw)
    place = jnp.arange(shards * cap, dtype=jnp.int32)
    home = (my_shard * cap + my_rank).astype(jnp.int32)
    ids = jnp.arange(positions, dtype=jnp.int32)
    return place, home, ids, [arrived]


def per_device(
    rows_in,
    norm_gain,
    kv_weight,
    queries,
    store_pages,
    passage_home,
    passage_ids,
    passage_count,
    recompute_rows,
):
    shards = lax.axis_size("store")
    me = lax.axis_index("store")
    owned, selected, _ = rows_in.shape
    local, plen = store_pages.shape[:2]
    ringed = shards == 4 * GROUP and lax.axis_size("parts") == 2 and kv_weight.shape[0] % 512 == 0
    rows = lax.dynamic_slice_in_dim(recompute_rows, me * owned, owned, 0)
    query_pos = query_positions(rows, plen)
    flat_rows = rows.reshape(-1)
    maxp = passage_ids.shape[1]
    if ringed:
        ids = lax.dynamic_slice_in_dim(passage_ids, me * owned, owned, 0).reshape(-1)
        small, (place, sources), terms = ring_plan(
            rows_in, norm_gain, kv_weight, store_pages, [ids, flat_rows, query_pos]
        )
        ids, flat_rows, query_pos = small
        pages = (place, passage_home, ids, sources)
        per_dev = local
    else:
        terms = gathered_projection(rows_in, norm_gain, kv_weight)
        pages = sent_pages(store_pages, passage_home, passage_ids)
        per_dev = 1
    part, stat, stacked = cached_attention(
        per_dev, maxp, plen, *pages, flat_rows, passage_count, queries, query_pos
    )
    terms = [t.reshape(-1, selected, t.shape[1]) for t in terms]
    half = len(terms) // 2
    weights, base = fresh_scores(
        maxp, passage_count, stacked, terms[:half], query_pos, part, stat
    )
    return fresh_attention(weights, terms[half:], base)


def solution(mesh):
    in_specs = (
        P(("parts", "store"), None, None),
        P(),
        P("store", None),
        P(("parts", "store"), None, None),
        P(("parts", "store"), None, None, None),
        P("parts"),
        P("parts", None),
        P(("parts", "store")),
        P("parts", None, None),
    )
    out_specs = P(("parts", "store"), None, None)
    return jax.shard_map(
        per_device, mesh=mesh, in_specs=in_specs, out_specs=out_specs, check_vma=False
    )
```
